512 devices in a mesh: tm: 16 (over y, x), space: 32 (over z, core).
Axes of the slice: x: 4, y: 4, z: 16, core: 2. Of those that a mesh axis runs over, the one named last changes fastest.
Arguments:
- lagrange: float32 [16, 4, 1024, 256], P('tm', None, 'space'), may hold values from -6 to 6
- obs_mult: float32 [16, 2, 4, 1024, 256], P('tm', None, None, 'space'), may hold values from -6 to 6
- increment: float32 [16, 4, 1024, 256], P('tm', None, 'space'), may hold values from -6 to 6
- model_side: float32 [16, 4, 1024, 256], P('tm', None, 'space'), may hold values from -6 to 6
- obs_side: float32 [16, 2, 4, 1024, 256], P('tm', None, None, 'space'), may hold values from -6 to 6
- model_var: float32 [16, 4, 1024, 256], P('tm', None, 'space'), may hold values from 0.5 to 2
- obs_var: float32 [16, 2, 4, 1024, 256], P('tm', None, None, 'space'), may hold values from 0.5 to 2
- courant_x: float32 [4, 1024, 256], P(None, 'space'), may hold values from -0.5 to 0.5
- courant_y: float32 [4, 1024, 256], P(None, 'space'), may hold values from -0.5 to 0.5
- diffusion: float32 [4, 1024, 256], P(None, 'space'), may hold values from 0.08 to 0.22
Outputs:
- lagrange_next: float32 [16, 4, 1024, 256], P('tm', None, 'space')
- obs_mult_next: float32 [16, 2, 4, 1024, 256], P('tm', None, None, 'space')
- increment_next: float32 [16, 4, 1024, 256], P('tm', None, 'space')
The draws below stay inside these ranges and needn't reach their ends.
All inputs are finite; a program needn't handle non-finite values.
Results may differ from the reference program's by a relative error of at most 0.000028.
Values sent between devices are 32-bit elements; how exact they have to be, the bound alone decides.
No kernel may reach another device: no remote copies, remote signals or barrier semaphores. Data moves between devices by JAX's collectives and lax.ppermute only.
A program may use at most 64 MiB of HBM per device.

```python
import math
import jax
import jax.numpy as jnp

LEV = 4
NY = 256
STEPS = 4
NW = 16
NX = 1024


def levels(key, extent, cuts, least, top_value):
    factor_of, own = 1.0, jax.random.fold_in(key, 6)
    for dim, shards_of in cuts:
        draws = jnp.exp(jax.random.uniform(jax.random.fold_in(own, dim), (shards_of,), jnp.float32, least / len(cuts), top_value / len(cuts)))
        factor_of = factor_of * jnp.repeat(draws, extent[dim] // shards_of).reshape([-1 if axis == dim else 1 for axis in range(len(extent))])
    return factor_of


def bell_draw(rng, extent, deviation, reach, shards=(), dtype=jnp.bfloat16):
    drawn = jax.random.normal(rng, extent, jnp.float32) * deviation
    if len(shards) > 0:
        drawn = levels(rng, extent, shards, -0.22, 0.18) * drawn
    return jnp.clip(drawn, min=-reach, max=reach).astype(dtype)


def setup_inputs(seed: int = 0) -> dict:
    key_of = jax.random.split(jax.random.key(seed), 11)
    lagrange = bell_draw(key_of[0], (NW, LEV, NX, NY), 1.0, 6.0, ((0, 16), (2, 32)), jnp.float32)
    obs_mult = bell_draw(key_of[1], (NW, 2, LEV, NX, NY), 1.0, 6.0, ((0, 16), (3, 32)), jnp.float32)
    increment = bell_draw(key_of[2], (NW, LEV, NX, NY), 1.0, 6.0, ((0, 16), (2, 32)), jnp.float32)
    model_side = bell_draw(key_of[3], (NW, LEV, NX, NY), 1.0, 6.0, ((0, 16), (2, 32)), jnp.float32)
    obs_side = bell_draw(key_of[4], (NW, 2, LEV, NX, NY), 1.0, 6.0, ((0, 16), (3, 32)), jnp.float32)
    model_var = jnp.clip(jnp.exp(math.log(2.0) - 1.3862944 * jax.random.uniform(key_of[5], (NW, LEV, NX, NY), jnp.float32) ** levels(key_of[5], (NW, LEV, NX, NY), ((0, 16), (2, 32)), -0.2, 0.2)), 0.5, 2.0)
    obs_var = jnp.clip(jnp.exp(math.log(2.0) - 1.3862944 * jax.random.uniform(key_of[6], (NW, 2, LEV, NX, NY), jnp.float32) ** levels(key_of[6], (NW, 2, LEV, NX, NY), ((0, 16), (3, 32)), -0.2, 0.2)), 0.5, 2.0)
    courant_x = jnp.clip(jax.random.uniform(key_of[7], (LEV, NX, NY), jnp.float32, -0.5, 0.5) * levels(key_of[7], (LEV, NX, NY), ((1, 32),), -0.4, 0.0), -0.5, 0.5)
    courant_y = jnp.clip(jax.random.uniform(key_of[8], (LEV, NX, NY), jnp.float32, -0.5, 0.5) * levels(key_of[8], (LEV, NX, NY), ((1, 32),), -0.4, 0.0), -0.5, 0.5)
    diffusion = jnp.clip(0.08 + 0.14 * jax.random.uniform(key_of[9], (LEV, NX, NY), jnp.float32) ** levels(key_of[9], (LEV, NX, NY), ((1, 32),), -0.2, 0.2), 0.08, 0.22)
    return {"lagrange": lagrange, "obs_mult": obs_mult, "increment": increment, "model_side": model_side, "obs_side": obs_side, "model_var": model_var, "obs_var": obs_var, "courant_x": courant_x, "courant_y": courant_y, "diffusion": diffusion}


def shift_north(field):
    return jnp.concatenate([field[..., 1:], jnp.zeros_like(field[..., :1])], axis=-1)


def shift_south(field):
    return jnp.concatenate([jnp.zeros_like(field[..., :1]), field[..., :-1]], axis=-1)


def tangent_step(field, courant_x, courant_y, diffusion):
    eastern = jnp.roll(field, -1, axis=-2)
    western = jnp.roll(field, 1, axis=-2)
    northern = shift_north(field)
    southern = shift_south(field)
    return (field - 0.5 * courant_x * (eastern - western) - 0.5 * courant_y * (northern - southern)
            + diffusion * (eastern + western + northern + southern - 4.0 * field))


def adjoint_step(field, courant_x, courant_y, diffusion):
    flux_x = courant_x * field
    flux_y = courant_y * field
    spread = diffusion * field
    return (field + 0.5 * (jnp.roll(flux_x, -1, axis=-2) - jnp.roll(flux_x, 1, axis=-2))
            + 0.5 * (shift_north(flux_y) - shift_south(flux_y))
            + jnp.roll(spread, -1, axis=-2) + jnp.roll(spread, 1, axis=-2)
            + shift_north(spread) + shift_south(spread) - 4.0 * spread)


def reference(lagrange, obs_mult, increment, model_side, obs_side, model_var, obs_var, courant_x, courant_y, diffusion):
    state = increment
    middle = state
    for step_index in range(STEPS):
        state = tangent_step(state, courant_x, courant_y, diffusion)
        if step_index == STEPS // 2 - 1:
            middle = state
    final = state
    previous = jnp.concatenate([jnp.zeros_like(final[:1]), final[:-1]], axis=0)
    resid_model = model_side - model_var * lagrange - (increment - previous)
    observed = jnp.stack([middle, final], axis=1)
    resid_obs = obs_side - obs_var * obs_mult - observed
    following = jnp.concatenate([lagrange[1:], jnp.zeros_like(lagrange[:1])], axis=0)
    pulled = obs_mult[:, 1] - following
    for step_index in range(STEPS):
        if step_index == STEPS // 2:
            pulled = pulled + obs_mult[:, 0]
        pulled = adjoint_step(pulled, courant_x, courant_y, diffusion)
    resid_state = -(lagrange + pulled)
    z_model = jnp.cumsum(resid_model, axis=0)
    z_obs = resid_obs / obs_var
    z_state = jnp.flip(jnp.cumsum(jnp.flip(resid_state, axis=0), axis=0), axis=0)
    cross_sum = jnp.sum(resid_model * z_model) + jnp.sum(resid_obs * z_obs) + jnp.sum(resid_state * z_state)
    square_sum = jnp.sum(z_model * z_model) + jnp.sum(z_obs * z_obs) + jnp.sum(z_state * z_state)
    step_len = cross_sum / (square_sum + 1e-6)
    return lagrange + step_len * z_model, obs_mult + step_len * z_obs, increment + step_len * z_state
```

```python
import functools

import jax
import jax.numpy as jnp
from jax import lax
from jax.experimental import pallas as pl
from jax.experimental.pallas import tpu as pltpu
from jax.sharding import PartitionSpec as P

STEPS = 4
LEV = 4
ROWS = 32
NY = 256
NW = 16
HALF = 128
EDGE = 7
F32 = jnp.float32

VMEM = pl.BlockSpec(memory_space=pltpu.VMEM)
ANY = pl.BlockSpec(memory_space=pl.ANY)


def call(kernel, out_shape, in_specs, out_specs, scratch=(), **kw):
    return pl.pallas_call(
        kernel,
        out_shape=out_shape,
        in_specs=in_specs,
        out_specs=out_specs,
        scratch_shapes=list(scratch),
        compiler_params=pltpu.CompilerParams(vmem_limit_bytes=16 * 1024 * 1024),
        **kw,
    )


def lower_half(shape):
    return lax.broadcasted_iota(jnp.int32, shape, 0) < 4


def pack_kernel(inc, obs, lag, cx, cy, df, first_out, last_out, first, last, sem):
    sources = [inc.at[0], obs.at[0, 1], obs.at[0, 0], lag.at[0], cx, cy, df]
    copies = []
    for f, src in enumerate(sources):
        copies.append(pltpu.make_async_copy(src.at[:, pl.ds(0, 8)], first.at[f], sem.at[2 * f]))
        copies.append(pltpu.make_async_copy(src.at[:, pl.ds(ROWS - 8, 8)], last.at[f], sem.at[2 * f + 1]))
    for c in copies:
        c.start()
    for c in copies:
        c.wait()
    low = lower_half((8, NY))
    for f in range(EDGE):
        for m in range(2):
            k = 8 * (2 * f + m)
            first_out[k : k + 8, :] = jnp.where(low, first[f, 2 * m], pltpu.roll(first[f, 2 * m + 1], 4, 0))
            last_out[k : k + 8, :] = jnp.where(low, pltpu.roll(last[f, 2 * m], 4, 0), last[f, 2 * m + 1])


def halo(nxt, prv, f, l):
    k = 8 * (2 * f + l // 2)
    low = lower_half((8, NY))
    a, b = nxt[k : k + 8, :], prv[k : k + 8, :]
    if l % 2 == 0:
        return jnp.where(low, a, pltpu.roll(b, 4, 0))
    return jnp.where(low, pltpu.roll(a, 4, 0), b)


def extend(core, nxt, prv, f, l):
    return jnp.concatenate([core, halo(nxt, prv, f, l)], axis=0)


def east(x):
    return pltpu.roll(x, ROWS + 7, 0)


def west(x):
    return pltpu.roll(x, 1, 0)


def north(x):
    return pltpu.roll(x, NY - 1, 1)


def south(x):
    return pltpu.roll(x, 1, 1)


def tangent(q, c):
    a0, ae, aw, an, as_ = c
    return a0 * q + ae * east(q) + aw * west(q) + an * north(q) + as_ * south(q)


def adjoint(p, c):
    a0, ae, aw, an, as_ = c
    return a0 * p + east(aw * p) + west(ae * p) + north(as_ * p) + south(an * p)


def run_kernel(inc, obs, lag, cx, cy, df, mside, mvar, oside, ovar, nxt, prv, send, zobs, part):
    col = lax.broadcasted_iota(jnp.int32, (ROWS + 8, NY), 1)
    cross = jnp.zeros((ROWS, NY), F32)
    square = jnp.zeros((ROWS, NY), F32)
    for l in range(LEV):
        ext = lambda core, f: extend(core, nxt, prv, f, l)
        x, y, d = ext(cx[l], 4), ext(cy[l], 5), ext(df[l], 6)
        x, y = 0.5 * x, 0.5 * y
        coefs = (
            1.0 - 4.0 * d,
            d - x,
            d + x,
            jnp.where(col == NY - 1, 0.0, d - y),
            jnp.where(col == 0, 0.0, d + y),
        )
        q = ext(inc[0, l], 0)
        for step in range(STEPS):
            q = tangent(q, coefs)
            if step == STEPS // 2 - 1:
                middle = q[:ROWS]
        final = q[:ROWS]
        p = ext(obs[0, 1, l], 1)
        b = ext(lag[0, l], 3)
        for step in range(STEPS):
            if step == STEPS // 2:
                p = p + ext(obs[0, 0, l], 2)
            p = adjoint(p, coefs)
            b = adjoint(b, coefs)
        lagr = lag[0, l]
        fixed = mside[0, l] - mvar[0, l] * lagr - inc[0, l]
        with_lag = lagr + p[:ROWS]
        b = b[:ROWS]
        for k in range(4):
            rows = slice(8 * k, 8 * k + 8)
            t = 4 * l + k
            send[t, 0:8, :] = fixed[rows]
            send[t, 8:16, :] = final[rows]
            send[t, 16:24, :] = with_lag[rows]
            send[t, 24:32, :] = b[rows]
        for j, state in enumerate((middle, final)):
            var = ovar[0, j, l]
            resid = oside[0, j, l] - var * obs[0, j, l] - state
            z = resid / var
            zobs[j, l] = z
            cross = cross + resid * z
            square = square + z * z
    fold = lambda v: v[0:8] + v[8:16] + v[16:24] + v[24:32]
    part[0] = fold(cross)
    part[1] = fold(square)


def sum_kernel(recv, part, back):
    cross, square = part[0], part[1]
    z = jnp.zeros((8, NY), F32)
    before = jnp.zeros((8, NY), F32)
    for w in range(NW):
        r = recv[w, 0:8, :] + before
        before = recv[w, 8:16, :]
        z = z + r
        cross = cross + r * z
        square = square + z * z
        back[w, 0:8, :] = z[:, :HALF]
        back[w, 8:16, :] = z[:, HALF:]
    z = jnp.zeros((8, NY), F32)
    after = jnp.zeros((8, NY), F32)
    for w in reversed(range(NW)):
        r = after - recv[w, 16:24, :]
        after = recv[w, 24:32, :]
        z = z + r
        cross = cross + r * z
        square = square + z * z
        back[w, 16:24, :] = z[:, :HALF]
        back[w, 24:32, :] = z[:, HALF:]

    def fold(v):
        v = v[:, :HALF] + v[:, HALF:]
        return v + pltpu.roll(v, HALF // 2, 1)

    lane = lax.broadcasted_iota(jnp.int32, (8, HALF), 1)
    both = jnp.where(lane < HALF // 2, fold(cross), fold(square))
    for w in range(NW):
        back[w, 32:40, :] = both


def scalar_kernel(count, recv, out):
    total = recv[0]
    for w in range(1, NW):
        total = total + recv[w]
    row = jnp.sum(total, axis=0, keepdims=True)
    for s in range(count):
        out[s] = row


def update_kernel(count, sums, recv, lag, obs, inc, zobs, lag_out, obs_out, inc_out):
    total = sums[0]
    for s in range(1, count):
        total = total + sums[s]
    lane = lax.broadcasted_iota(jnp.int32, (1, HALF), 1)
    cross = jnp.sum(jnp.where(lane < HALF // 2, total, 0.0), axis=1, keepdims=True)
    square = jnp.sum(jnp.where(lane < HALF // 2, 0.0, total), axis=1, keepdims=True)
    step = cross / (square + 1e-06)
    for l in range(LEV):
        for k in range(4):
            rows = slice(8 * k, 8 * k + 8)
            t = 4 * l + k
            for h in range(2):
                cols = slice(HALF * h, HALF * h + HALF)
                lag_out[0, l, rows, cols] = lag[0, l, rows, cols] + step * recv[t, 8 * h : 8 * h + 8, :]
                inc_out[0, l, rows, cols] = inc[0, l, rows, cols] + step * recv[t, 16 + 8 * h : 24 + 8 * h, :]
        for j in range(2):
            obs_out[0, j, l] = obs[0, j, l] + step * zobs[j, l]


def body(lag, obs, inc, mside, oside, mvar, ovar, cx, cy, df):
    sds = jax.ShapeDtypeStruct
    size = lax.axis_size("space")
    edge = sds((EDGE * LEV * 4, NY), F32)
    first, last = call(
        pack_kernel,
        (edge, edge),
        [ANY] * 6,
        (VMEM, VMEM),
        [
            pltpu.VMEM((EDGE, LEV, 8, NY), F32),
            pltpu.VMEM((EDGE, LEV, 8, NY), F32),
            pltpu.SemaphoreType.DMA((2 * EDGE,)),
        ],
        name="pack_edges",
    )(inc, obs, lag, cx, cy, df)
    nxt = lax.ppermute(first, "space", [((i + 1) % size, i) for i in range(size)])
    prv = lax.ppermute(last, "space", [(i, (i + 1) % size) for i in range(size)])
    send, zobs, part = call(
        run_kernel,
        (sds((NW, 32, NY), F32), sds((2, LEV, ROWS, NY), F32), sds((2, 8, NY), F32)),
        [VMEM] * 12,
        (VMEM, VMEM, VMEM),
        name="stencil_runs",
    )(inc, obs, lag, cx, cy, df, mside, mvar, oside, ovar, nxt, prv)
    recv = lax.all_to_all(send, "tm", 0, 0)
    back = call(sum_kernel, sds((NW, 40, HALF), F32), [VMEM] * 2, VMEM, name="window_sums")(recv, part)
    back = lax.all_to_all(back, "tm", 0, 0)
    sums = call(
        functools.partial(scalar_kernel, size),
        sds((size, 1, HALF), F32),
        [pl.BlockSpec((NW, 8, HALF), lambda i: (0, 4, 0))],
        pl.BlockSpec((size, 1, HALF), lambda i: (0, 0, 0)),
        grid=(1,),
        name="scalars",
    )(back)
    sums = lax.all_to_all(sums, "space", 0, 0)
    return call(
        functools.partial(update_kernel, size),
        (sds(lag.shape, F32), sds(obs.shape, F32), sds(inc.shape, F32)),
        [VMEM] * 6,
        (VMEM, VMEM, VMEM),
        name="update",
    )(sums, back, lag, obs, inc, zobs)


def solution(mesh):
    field = P("tm", None, "space", None)
    pair = P("tm", None, None, "space", None)
    coef = P(None, "space", None)
    return jax.shard_map(
        body,
        mesh=mesh,
        in_specs=(field, pair, field, field, pair, field, pair, coef, coef, coef),
        out_specs=(field, pair, field),
        check_vma=False,
    )
```

```python
import functools

import jax
import jax.numpy as jnp
from jax import lax
from jax.experimental import pallas as pl
from jax.experimental.pallas import tpu as pltpu
from jax.sharding import PartitionSpec as P

STEPS = 4
LEV = 4
ROWS = 32
NY = 256
NW = 16
HALF = 128
EDGE = 7
F32 = jnp.float32

VMEM = pl.BlockSpec(memory_space=pltpu.VMEM)
ANY = pl.BlockSpec(memory_space=pl.ANY)


def call(kernel, out_shape, in_specs, out_specs, scratch=(), **kw):
    return pl.pallas_call(
        kernel,
        out_shape=out_shape,
        in_specs=in_specs,
        out_specs=out_specs,
        scratch_shapes=list(scratch),
        compiler_params=pltpu.CompilerParams(vmem_limit_bytes=16 * 1024 * 1024),
        **kw,
    )


def lower_half(shape):
    return lax.broadcasted_iota(jnp.int32, shape, 0) < 4


def fetch_kernel(*refs):
    args, (first_out, last_out), copies_out = refs[:10], refs[10:12], refs[12:22]
    first, last, edge_sem, bulk_sem = refs[22:]
    lag, obs, inc, _, _, _, _, cx, cy, df = args
    sources = [inc.at[0], obs.at[0, 1], obs.at[0, 0], lag.at[0], cx, cy, df]
    edges = []
    for f, src in enumerate(sources):
        edges.append(pltpu.make_async_copy(src.at[:, pl.ds(0, 8)], first.at[f], edge_sem.at[2 * f]))
        edges.append(pltpu.make_async_copy(src.at[:, pl.ds(ROWS - 8, 8)], last.at[f], edge_sem.at[2 * f + 1]))
    bulk = [pltpu.make_async_copy(src, dst, bulk_sem.at[i]) for i, (src, dst) in enumerate(zip(args, copies_out))]
    for c in edges + bulk:
        c.start()
    for c in edges:
        c.wait()
    low = lower_half((8, NY))
    for f in range(EDGE):
        for m in range(2):
            k = 8 * (2 * f + m)
            first_out[k : k + 8, :] = jnp.where(low, first[f, 2 * m], pltpu.roll(first[f, 2 * m + 1], 4, 0))
            last_out[k : k + 8, :] = jnp.where(low, pltpu.roll(last[f, 2 * m], 4, 0), last[f, 2 * m + 1])
    for c in bulk:
        c.wait()


def halo(nxt, prv, f, l):
    k = 8 * (2 * f + l // 2)
    low = lower_half((8, NY))
    a, b = nxt[k : k + 8, :], prv[k : k + 8, :]
    if l % 2 == 0:
        return jnp.where(low, a, pltpu.roll(b, 4, 0))
    return jnp.where(low, pltpu.roll(a, 4, 0), b)


def extend(core, nxt, prv, f, l):
    return jnp.concatenate([core, halo(nxt, prv, f, l)], axis=0)


def east(x):
    return pltpu.roll(x, ROWS + 7, 0)


def west(x):
    return pltpu.roll(x, 1, 0)


def north(x):
    return pltpu.roll(x, NY - 1, 1)


def south(x):
    return pltpu.roll(x, 1, 1)


def tangent(q, c):
    a0, ae, aw, an, as_ = c
    return a0 * q + ae * east(q) + aw * west(q) + an * north(q) + as_ * south(q)


def adjoint(p, c):
    a0, ae, aw, an, as_ = c
    return a0 * p + east(aw * p) + west(ae * p) + north(as_ * p) + south(an * p)


def run_kernel(inc, obs, lag, cx, cy, df, mside, mvar, oside, ovar, nxt, prv, send, zobs, part):
    col = lax.broadcasted_iota(jnp.int32, (ROWS + 8, NY), 1)
    cross = jnp.zeros((ROWS, NY), F32)
    square = jnp.zeros((ROWS, NY), F32)
    for l in range(LEV):
        ext = lambda core, f: extend(core, nxt, prv, f, l)
        x, y, d = ext(cx[l], 4), ext(cy[l], 5), ext(df[l], 6)
        x, y = 0.5 * x, 0.5 * y
        coefs = (
            1.0 - 4.0 * d,
            d - x,
            d + x,
            jnp.where(col == NY - 1, 0.0, d - y),
            jnp.where(col == 0, 0.0, d + y),
        )
        q = ext(inc[0, l], 0)
        for step in range(STEPS):
            q = tangent(q, coefs)
            if step == STEPS // 2 - 1:
                middle = q[:ROWS]
        final = q[:ROWS]
        p = ext(obs[0, 1, l], 1)
        b = ext(lag[0, l], 3)
        for step in range(STEPS):
            if step == STEPS // 2:
                p = p + ext(obs[0, 0, l], 2)
            p = adjoint(p, coefs)
            b = adjoint(b, coefs)
        lagr = lag[0, l]
        fixed = mside[0, l] - mvar[0, l] * lagr - inc[0, l]
        with_lag = lagr + p[:ROWS]
        b = b[:ROWS]
        for k in range(4):
            rows = slice(8 * k, 8 * k + 8)
            t = 4 * l + k
            send[t, 0:8, :] = fixed[rows]
            send[t, 8:16, :] = final[rows]
            send[t, 16:24, :] = with_lag[rows]
            send[t, 24:32, :] = b[rows]
        for j, state in enumerate((middle, final)):
            var = ovar[0, j, l]
            resid = oside[0, j, l] - var * obs[0, j, l] - state
            z = resid / var
            zobs[j, l] = z
            cross = cross + resid * z
            square = square + z * z
    fold = lambda v: v[0:8] + v[8:16] + v[16:24] + v[24:32]
    part[0] = fold(cross)
    part[1] = fold(square)


def sum_kernel(recv, part, back):
    cross, square = part[0], part[1]
    z = jnp.zeros((8, NY), F32)
    before = jnp.zeros((8, NY), F32)
    for w in range(NW):
        r = recv[w, 0:8, :] + before
        before = recv[w, 8:16, :]
        z = z + r
        cross = cross + r * z
        square = square + z * z
        back[w, 0:8, :] = z[:, :HALF]
        back[w, 8:16, :] = z[:, HALF:]
    z = jnp.zeros((8, NY), F32)
    after = jnp.zeros((8, NY), F32)
    for w in reversed(range(NW)):
        r = after - recv[w, 16:24, :]
        after = recv[w, 24:32, :]
        z = z + r
        cross = cross + r * z
        square = square + z * z
        back[w, 16:24, :] = z[:, :HALF]
        back[w, 24:32, :] = z[:, HALF:]

    def fold(v):
        v = v[:, :HALF] + v[:, HALF:]
        return v + pltpu.roll(v, HALF // 2, 1)

    lane = lax.broadcasted_iota(jnp.int32, (8, HALF), 1)
    both = jnp.where(lane < HALF // 2, fold(cross), fold(square))
    for w in range(NW):
        back[w, 32:40, :] = both


def scalar_kernel(count, recv, out):
    total = recv[0]
    for w in range(1, NW):
        total = total + recv[w]
    row = jnp.sum(total, axis=0, keepdims=True)
    for s in range(count):
        out[s] = row


def update_kernel(count, sums, recv, lag, obs, inc, zobs, lag_out, obs_out, inc_out):
    total = sums[0]
    for s in range(1, count):
        total = total + sums[s]
    lane = lax.broadcasted_iota(jnp.int32, (1, HALF), 1)
    cross = jnp.sum(jnp.where(lane < HALF // 2, total, 0.0), axis=1, keepdims=True)
    square = jnp.sum(jnp.where(lane < HALF // 2, 0.0, total), axis=1, keepdims=True)
    step = cross / (square + 1e-06)
    for l in range(LEV):
        for k in range(4):
            rows = slice(8 * k, 8 * k + 8)
            t = 4 * l + k
            for h in range(2):
                cols = slice(HALF * h, HALF * h + HALF)
                lag_out[0, l, rows, cols] = lag[0, l, rows, cols] + step * recv[t, 8 * h : 8 * h + 8, :]
                inc_out[0, l, rows, cols] = inc[0, l, rows, cols] + step * recv[t, 16 + 8 * h : 24 + 8 * h, :]
        for j in range(2):
            obs_out[0, j, l] = obs[0, j, l] + step * zobs[j, l]


def body(lag, obs, inc, mside, oside, mvar, ovar, cx, cy, df):
    sds = jax.ShapeDtypeStruct
    size = lax.axis_size("space")
    edge = sds((EDGE * LEV * 4, NY), F32)
    args = (lag, obs, inc, mside, oside, mvar, ovar, cx, cy, df)
    args = [pltpu.with_memory_space_constraint(x, pltpu.HBM) for x in args]
    first, last, lag, obs, inc, mside, oside, mvar, ovar, cx, cy, df = call(
        fetch_kernel,
        (edge, edge) + tuple(sds(x.shape, F32) for x in args),
        [ANY] * 10,
        (VMEM,) * 12,
        [
            pltpu.VMEM((EDGE, LEV, 8, NY), F32),
            pltpu.VMEM((EDGE, LEV, 8, NY), F32),
            pltpu.SemaphoreType.DMA((2 * EDGE,)),
            pltpu.SemaphoreType.DMA((10,)),
        ],
        name="fetch",
    )(*args)
    nxt = lax.ppermute(first, "space", [((i + 1) % size, i) for i in range(size)])
    prv = lax.ppermute(last, "space", [(i, (i + 1) % size) for i in range(size)])
    send, zobs, part = call(
        run_kernel,
        (sds((NW, 32, NY), F32), sds((2, LEV, ROWS, NY), F32), sds((2, 8, NY), F32)),
        [VMEM] * 12,
        (VMEM, VMEM, VMEM),
        name="stencil_runs",
    )(inc, obs, lag, cx, cy, df, mside, mvar, oside, ovar, nxt, prv)
    recv = lax.all_to_all(send, "tm", 0, 0)
    back = call(sum_kernel, sds((NW, 40, HALF), F32), [VMEM] * 2, VMEM, name="window_sums")(recv, part)
    back = lax.all_to_all(back, "tm", 0, 0)
    sums = call(
        functools.partial(scalar_kernel, size),
        sds((size, 1, HALF), F32),
        [pl.BlockSpec((NW, 8, HALF), lambda i: (0, 4, 0))],
        pl.BlockSpec((size, 1, HALF), lambda i: (0, 0, 0)),
        grid=(1,),
        name="scalars",
    )(back)
    sums = lax.all_to_all(sums, "space", 0, 0)
    return call(
        functools.partial(update_kernel, size),
        (sds(lag.shape, F32), sds(obs.shape, F32), sds(inc.shape, F32)),
        [VMEM] * 6,
        (VMEM, VMEM, VMEM),
        name="update",
    )(sums, back, lag, obs, inc, zobs)


def solution(mesh):
    field = P("tm", None, "space", None)
    pair = P("tm", None, None, "space", None)
    coef = P(None, "space", None)
    return jax.shard_map(
        body,
        mesh=mesh,
        in_specs=(field, pair, field, field, pair, field, pair, coef, coef, coef),
        out_specs=(field, pair, field),
        check_vma=False,
    )
```

```python
import functools

import jax
import jax.numpy as jnp
from jax import lax
from jax.experimental import pallas as pl
from jax.experimental.pallas import tpu as pltpu
from jax.sharding import PartitionSpec as P

STEPS = 4
LEV = 4
ROWS = 32
NY = 256
NW = 16
HALF = 128
EDGE = 7
F32 = jnp.float32

VMEM = pl.BlockSpec(memory_space=pltpu.VMEM)
ANY = pl.BlockSpec(memory_space=pl.ANY)


def call(kernel, out_shape, in_specs, out_specs, scratch=(), **kw):
    return pl.pallas_call(
        kernel,
        out_shape=out_shape,
        in_specs=in_specs,
        out_specs=out_specs,
        scratch_shapes=list(scratch),
        compiler_params=pltpu.CompilerParams(vmem_limit_bytes=16 * 1024 * 1024),
        **kw,
    )


def lower_half(shape):
    return lax.broadcasted_iota(jnp.int32, shape, 0) < 4


def edge_kernel(lag, obs, inc, cx, cy, df, first_out, last_out, first, last, sem):
    sources = [inc.at[0], obs.at[0, 1], obs.at[0, 0], lag.at[0], cx, cy, df]
    copies = []
    for f, src in enumerate(sources):
        copies.append(pltpu.make_async_copy(src.at[:, pl.ds(0, 8)], first.at[f], sem.at[2 * f]))
        copies.append(pltpu.make_async_copy(src.at[:, pl.ds(ROWS - 8, 8)], last.at[f], sem.at[2 * f + 1]))
    for c in copies:
        c.start()
    for c in copies:
        c.wait()
    low = lower_half((8, NY))
    for f in range(EDGE):
        for m in range(2):
            k = 8 * (2 * f + m)
            first_out[k : k + 8, :] = jnp.where(low, first[f, 2 * m], pltpu.roll(first[f, 2 * m + 1], 4, 0))
            last_out[k : k + 8, :] = jnp.where(low, pltpu.roll(last[f, 2 * m], 4, 0), last[f, 2 * m + 1])


def halo(nxt, prv, f, l):
    k = 8 * (2 * f + l // 2)
    low = lower_half((8, NY))
    a, b = nxt[k : k + 8, :], prv[k : k + 8, :]
    if l % 2 == 0:
        return jnp.where(low, a, pltpu.roll(b, 4, 0))
    return jnp.where(low, pltpu.roll(a, 4, 0), b)


def east(x):
    return pltpu.roll(x, x.shape[0] - 1, 0)


def west(x):
    return pltpu.roll(x, 1, 0)


def north(x):
    return pltpu.roll(x, NY - 1, 1)


def south(x):
    return pltpu.roll(x, 1, 1)


def tangent(q, c):
    a0, ae, aw, an, as_ = c
    return a0 * q + ae * east(q) + aw * west(q) + an * north(q) + as_ * south(q)


def adjoint(p, c):
    a0, ae, aw, an, as_ = c
    return a0 * p + east(aw * p) + west(ae * p) + north(as_ * p) + south(an * p)


def runs(inc, obs1, obs0, lag, x, y, d):
    col = lax.broadcasted_iota(jnp.int32, d.shape, 1)
    x, y = 0.5 * x, 0.5 * y
    coefs = (
        1.0 - 4.0 * d,
        d - x,
        d + x,
        jnp.where(col == NY - 1, 0.0, d - y),
        jnp.where(col == 0, 0.0, d + y),
    )
    q, p, b = inc, obs1, lag
    for step in range(STEPS):
        if step == STEPS // 2:
            middle = q
            p = p + obs0
        q = tangent(q, coefs)
        p = adjoint(p, coefs)
        b = adjoint(b, coefs)
    return middle, q, p, b


def inner_kernel(lag, obs, inc, mside, oside, mvar, ovar, cx, cy, df, fixed, states, resid, inverse):
    for l in range(LEV):
        lagr = lag[0, l]
        out = runs(inc[0, l], obs[0, 1, l], obs[0, 0, l], lagr, cx[l], cy[l], df[l])
        for i in range(4):
            states[i, l] = out[i] + lagr if i == 2 else out[i]
        fixed[l] = mside[0, l] - mvar[0, l] * lagr - inc[0, l]
        for j in range(2):
            var = ovar[0, j, l]
            resid[j, l] = oside[0, j, l] - var * obs[0, j, l]
            inverse[j, l] = 1.0 / var


def outer_kernel(first, last, nxt, prv, fixed, states, resid, inverse, send, zobs, part):
    low = lower_half((8, NY))
    cross = jnp.zeros((8, NY), F32)
    square = jnp.zeros((8, NY), F32)
    for l in range(LEV):
        ring = [jnp.concatenate([last[f, l], halo(nxt, prv, f, l), first[f, l]], axis=0) for f in range(EDGE)]
        out = list(runs(*ring))
        out[2] = out[2] + ring[3]
        for k in range(4):
            rows = slice(8 * k, 8 * k + 8)
            tiles = [states[i, l, rows, :] for i in range(4)]
            if k == 0:
                tiles = [jnp.where(low, o[16:24], v) for o, v in zip(out, tiles)]
            if k == 3:
                tiles = [jnp.where(low, v, o[0:8]) for o, v in zip(out, tiles)]
            t = 4 * l + k
            send[t, 0:8, :] = fixed[l, rows, :]
            for i in range(1, 4):
                send[t, 8 * i : 8 * i + 8, :] = tiles[i]
            for j in range(2):
                r = resid[j, l, rows, :] - tiles[j]
                z = r * inverse[j, l, rows, :]
                zobs[j, l, rows, :] = z
                cross = cross + r * z
                square = square + z * z
    part[0] = cross
    part[1] = square


def sum_kernel(recv, part, back):
    cross, square = part[0], part[1]
    z = jnp.zeros((8, NY), F32)
    before = jnp.zeros((8, NY), F32)
    for w in range(NW):
        r = recv[w, 0:8, :] + before
        before = recv[w, 8:16, :]
        z = z + r
        cross = cross + r * z
        square = square + z * z
        back[w, 0:8, :] = z[:, :HALF]
        back[w, 8:16, :] = z[:, HALF:]
    z = jnp.zeros((8, NY), F32)
    after = jnp.zeros((8, NY), F32)
    for w in reversed(range(NW)):
        r = after - recv[w, 16:24, :]
        after = recv[w, 24:32, :]
        z = z + r
        cross = cross + r * z
        square = square + z * z
        back[w, 16:24, :] = z[:, :HALF]
        back[w, 24:32, :] = z[:, HALF:]

    def fold(v):
        v = v[:, :HALF] + v[:, HALF:]
        return v + pltpu.roll(v, HALF // 2, 1)

    lane = lax.broadcasted_iota(jnp.int32, (8, HALF), 1)
    both = jnp.where(lane < HALF // 2, fold(cross), fold(square))
    for w in range(NW):
        back[w, 32:40, :] = both


def scalar_kernel(count, recv, out):
    total = recv[0]
    for w in range(1, NW):
        total = total + recv[w]
    row = jnp.sum(total, axis=0, keepdims=True)
    for s in range(count):
        out[s] = row


def update_kernel(count, sums, recv, lag, obs, inc, zobs, lag_out, obs_out, inc_out):
    total = sums[0]
    for s in range(1, count):
        total = total + sums[s]
    lane = lax.broadcasted_iota(jnp.int32, (1, HALF), 1)
    cross = jnp.sum(jnp.where(lane < HALF // 2, total, 0.0), axis=1, keepdims=True)
    square = jnp.sum(jnp.where(lane < HALF // 2, 0.0, total), axis=1, keepdims=True)
    step = cross / (square + 1e-06)
    for l in range(LEV):
        for k in range(4):
            rows = slice(8 * k, 8 * k + 8)
            t = 4 * l + k
            for h in range(2):
                cols = slice(HALF * h, HALF * h + HALF)
                lag_out[0, l, rows, cols] = lag[0, l, rows, cols] + step * recv[t, 8 * h : 8 * h + 8, :]
                inc_out[0, l, rows, cols] = inc[0, l, rows, cols] + step * recv[t, 16 + 8 * h : 24 + 8 * h, :]
        for j in range(2):
            obs_out[0, j, l] = obs[0, j, l] + step * zobs[j, l]


def body(lag, obs, inc, mside, oside, mvar, ovar, cx, cy, df):
    sds = jax.ShapeDtypeStruct
    size = lax.axis_size("space")
    edge = sds((EDGE * LEV * 4, NY), F32)
    tiles = sds((EDGE, LEV, 8, NY), F32)
    one, two, four = (sds(n + (LEV, ROWS, NY), F32) for n in ((), (2,), (4,)))
    held = [pltpu.with_memory_space_constraint(x, pltpu.HBM) for x in (lag, obs, inc, mside, oside, mvar, ovar, cx, cy, df)]
    first, last, first_tiles, last_tiles = call(
        edge_kernel,
        (edge, edge, tiles, tiles),
        [ANY] * 6,
        (VMEM,) * 4,
        [pltpu.SemaphoreType.DMA((2 * EDGE,))],
        name="edges",
    )(*held[:3], *held[7:])
    nxt = lax.ppermute(first, "space", [((i + 1) % size, i) for i in range(size)])
    prv = lax.ppermute(last, "space", [(i, (i + 1) % size) for i in range(size)])
    inner = call(
        inner_kernel,
        (one, four, two, two),
        [VMEM] * 10,
        (VMEM,) * 4,
        name="inner_runs",
        cost_estimate=pl.CostEstimate(flops=8 * 1024 * 1024, bytes_accessed=4 * 1024 * 1024, transcendentals=0),
    )(*held)
    send, zobs, part = call(
        outer_kernel,
        (sds((NW, 32, NY), F32), two, sds((2, 8, NY), F32)),
        [VMEM] * 8,
        (VMEM, VMEM, VMEM),
        name="outer_runs",
    )(first_tiles, last_tiles, nxt, prv, *inner)
    recv = lax.all_to_all(send, "tm", 0, 0)
    back = call(sum_kernel, sds((NW, 40, HALF), F32), [VMEM] * 2, VMEM, name="window_sums")(recv, part)
    back = lax.all_to_all(back, "tm", 0, 0)
    sums = call(
        functools.partial(scalar_kernel, size),
        sds((size, 1, HALF), F32),
        [pl.BlockSpec((NW, 8, HALF), lambda i: (0, 4, 0))],
        pl.BlockSpec((size, 1, HALF), lambda i: (0, 0, 0)),
        grid=(1,),
        name="scalars",
    )(back)
    sums = lax.all_to_all(sums, "space", 0, 0)
    return call(
        functools.partial(update_kernel, size),
        (sds(lag.shape, F32), sds(obs.shape, F32), sds(inc.shape, F32)),
        [VMEM] * 6,
        (VMEM, VMEM, VMEM),
        name="update",
    )(sums, back, lag, obs, inc, zobs)


def solution(mesh):
    field = P("tm", None, "space", None)
    pair = P("tm", None, None, "space", None)
    coef = P(None, "space", None)
    return jax.shard_map(
        body,
        mesh=mesh,
        in_specs=(field, pair, field, field, pair, field, pair, coef, coef, coef),
        out_specs=(field, pair, field),
        check_vma=False,
    )
```

```python
import functools

import jax
import jax.numpy as jnp
from jax import lax
from jax.experimental import pallas as pl
from jax.experimental.pallas import tpu as pltpu
from jax.sharding import PartitionSpec as P

STEPS = 4
LEV = 4
ROWS = 32
NY = 256
NW = 16
HALF = 128
EDGE = 7
F32 = jnp.float32

VMEM = pl.BlockSpec(memory_space=pltpu.VMEM)
ANY = pl.BlockSpec(memory_space=pl.ANY)


def call(kernel, out_shape, in_specs, out_specs, scratch=(), **kw):
    return pl.pallas_call(
        kernel,
        out_shape=out_shape,
        in_specs=in_specs,
        out_specs=out_specs,
        scratch_shapes=list(scratch),
        compiler_params=pltpu.CompilerParams(vmem_limit_bytes=16 * 1024 * 1024),
        **kw,
    )


def lower_half(shape):
    return lax.broadcasted_iota(jnp.int32, shape, 0) < 4


def edge_kernel(lag, obs, inc, cx, cy, df, first_out, last_out, first, last, sem):
    sources = [inc.at[0], obs.at[0, 1], obs.at[0, 0], lag.at[0], cx, cy, df]
    copies = []
    for f, src in enumerate(sources):
        copies.append(pltpu.make_async_copy(src.at[:, pl.ds(0, 8)], first.at[f], sem.at[2 * f]))
        copies.append(pltpu.make_async_copy(src.at[:, pl.ds(ROWS - 8, 8)], last.at[f], sem.at[2 * f + 1]))
    for c in copies:
        c.start()
    for c in copies:
        c.wait()
    low = lower_half((8, NY))
    for f in range(EDGE):
        for m in range(2):
            k = 8 * (2 * f + m)
            first_out[k : k + 8, :] = jnp.where(low, first[f, 2 * m], pltpu.roll(first[f, 2 * m + 1], 4, 0))
            last_out[k : k + 8, :] = jnp.where(low, pltpu.roll(last[f, 2 * m], 4, 0), last[f, 2 * m + 1])


def halo(nxt, prv, f, l):
    k = 8 * (2 * f + l // 2)
    low = lower_half((8, NY))
    a, b = nxt[k : k + 8, :], prv[k : k + 8, :]
    if l % 2 == 0:
        return jnp.where(low, a, pltpu.roll(b, 4, 0))
    return jnp.where(low, pltpu.roll(a, 4, 0), b)


def east(x):
    return pltpu.roll(x, x.shape[0] - 1, 0)


def west(x):
    return pltpu.roll(x, 1, 0)


def north(x):
    return pltpu.roll(x, NY - 1, 1)


def south(x):
    return pltpu.roll(x, 1, 1)


def tangent(q, c):
    a0, ae, aw, an, as_ = c
    return a0 * q + ae * east(q) + aw * west(q) + an * north(q) + as_ * south(q)


def adjoint(p, c):
    a0, ae, aw, an, as_ = c
    return a0 * p + east(aw * p) + west(ae * p) + north(as_ * p) + south(an * p)


def runs(inc, obs1, obs0, lag, x, y, d):
    col = lax.broadcasted_iota(jnp.int32, d.shape, 1)
    x, y = 0.5 * x, 0.5 * y
    coefs = (
        1.0 - 4.0 * d,
        d - x,
        d + x,
        jnp.where(col == NY - 1, 0.0, d - y),
        jnp.where(col == 0, 0.0, d + y),
    )
    q, p, b = inc, obs1, lag
    for step in range(STEPS):
        if step == STEPS // 2:
            middle = q
            p = p + obs0
        q = tangent(q, coefs)
        p = adjoint(p, coefs)
        b = adjoint(b, coefs)
    return middle, q, p, b


def inner_kernel(lag, obs, inc, mside, oside, mvar, ovar, cx, cy, df, fixed, states, resid, inverse):
    for l in range(LEV):
        lagr = lag[0, l]
        out = runs(inc[0, l], obs[0, 1, l], obs[0, 0, l], lagr, cx[l], cy[l], df[l])
        for i in range(4):
            states[i, l] = out[i] + lagr if i == 2 else out[i]
        fixed[l] = mside[0, l] - mvar[0, l] * lagr - inc[0, l]
        for j in range(2):
            var = ovar[0, j, l]
            resid[j, l] = oside[0, j, l] - var * obs[0, j, l]
            inverse[j, l] = 1.0 / var


def outer_kernel(first, last, nxt, prv, fixed, states, resid, inverse, send, zobs, part):
    low = lower_half((8, NY))
    cross = jnp.zeros((8, NY), F32)
    square = jnp.zeros((8, NY), F32)
    for l in range(LEV):
        ring = [jnp.concatenate([last[f, l], halo(nxt, prv, f, l), first[f, l]], axis=0) for f in range(EDGE)]
        out = list(runs(*ring))
        out[2] = out[2] + ring[3]
        for k in range(4):
            rows = slice(8 * k, 8 * k + 8)
            tiles = [states[i, l, rows, :] for i in range(4)]
            if k == 0:
                tiles = [jnp.where(low, o[16:24], v) for o, v in zip(out, tiles)]
            if k == 3:
                tiles = [jnp.where(low, v, o[0:8]) for o, v in zip(out, tiles)]
            t = 4 * l + k
            send[t, 0:8, :] = fixed[l, rows, :]
            for i in range(1, 4):
                send[t, 8 * i : 8 * i + 8, :] = tiles[i]
            for j in range(2):
                r = resid[j, l, rows, :] - tiles[j]
                z = r * inverse[j, l, rows, :]
                zobs[j, l, rows, :] = z
                cross = cross + r * z
                square = square + z * z
    part[0] = cross
    part[1] = square


def sum_kernel(count, recv, part, back, out):
    cross, square = part[0], part[1]
    z = jnp.zeros((8, NY), F32)
    before = jnp.zeros((8, NY), F32)
    for w in range(NW):
        r = recv[w, 0:8, :] + before
        before = recv[w, 8:16, :]
        z = z + r
        cross = cross + r * z
        square = square + z * z
        back[w, 0:8, :] = z[:, :HALF]
        back[w, 8:16, :] = z[:, HALF:]
    z = jnp.zeros((8, NY), F32)
    after = jnp.zeros((8, NY), F32)
    for w in reversed(range(NW)):
        r = after - recv[w, 16:24, :]
        after = recv[w, 24:32, :]
        z = z + r
        cross = cross + r * z
        square = square + z * z
        back[w, 16:24, :] = z[:, :HALF]
        back[w, 24:32, :] = z[:, HALF:]

    def fold(v):
        v = v[:, :HALF] + v[:, HALF:]
        return v + pltpu.roll(v, HALF // 2, 1)

    lane = lax.broadcasted_iota(jnp.int32, (8, HALF), 1)
    both = jnp.where(lane < HALF // 2, fold(cross), fold(square))
    row = jnp.sum(both, axis=0, keepdims=True)
    for s in range(count):
        out[s] = row


def join_kernel(count, sums, back, out):
    total = sums[0]
    for s in range(1, count):
        total = total + sums[s]
    tile = jnp.broadcast_to(total, (8, HALF))
    for w in range(NW):
        out[w, 0:32, :] = back[w]
        out[w, 32:40, :] = tile


def update_kernel(recv, lag, obs, inc, zobs, lag_out, obs_out, inc_out):
    total = recv[0, 32:33, :]
    for w in range(1, NW):
        total = total + recv[w, 32:33, :]
    lane = lax.broadcasted_iota(jnp.int32, (1, HALF), 1)
    cross = jnp.sum(jnp.where(lane < HALF // 2, total, 0.0), axis=1, keepdims=True)
    square = jnp.sum(jnp.where(lane < HALF // 2, 0.0, total), axis=1, keepdims=True)
    step = cross / (square + 1e-06)
    for l in range(LEV):
        for k in range(4):
            rows = slice(8 * k, 8 * k + 8)
            t = 4 * l + k
            for h in range(2):
                cols = slice(HALF * h, HALF * h + HALF)
                lag_out[0, l, rows, cols] = lag[0, l, rows, cols] + step * recv[t, 8 * h : 8 * h + 8, :]
                inc_out[0, l, rows, cols] = inc[0, l, rows, cols] + step * recv[t, 16 + 8 * h : 24 + 8 * h, :]
        for j in range(2):
            obs_out[0, j, l] = obs[0, j, l] + step * zobs[j, l]


def body(lag, obs, inc, mside, oside, mvar, ovar, cx, cy, df):
    sds = jax.ShapeDtypeStruct
    size = lax.axis_size("space")
    edge = sds((EDGE * LEV * 4, NY), F32)
    tiles = sds((EDGE, LEV, 8, NY), F32)
    one, two, four = (sds(n + (LEV, ROWS, NY), F32) for n in ((), (2,), (4,)))
    held = [pltpu.with_memory_space_constraint(x, pltpu.HBM) for x in (lag, obs, inc, mside, oside, mvar, ovar, cx, cy, df)]
    first, last, first_tiles, last_tiles = call(
        edge_kernel,
        (edge, edge, tiles, tiles),
        [ANY] * 6,
        (VMEM,) * 4,
        [pltpu.SemaphoreType.DMA((2 * EDGE,))],
        name="edges",
    )(*held[:3], *held[7:])
    nxt = lax.ppermute(first, "space", [((i + 1) % size, i) for i in range(size)])
    prv = lax.ppermute(last, "space", [(i, (i + 1) % size) for i in range(size)])
    inner = call(
        inner_kernel,
        (one, four, two, two),
        [VMEM] * 10,
        (VMEM,) * 4,
        name="inner_runs",
        cost_estimate=pl.CostEstimate(flops=8 * 1024 * 1024, bytes_accessed=4 * 1024 * 1024, transcendentals=0),
    )(*held)
    send, zobs, part = call(
        outer_kernel,
        (sds((NW, 32, NY), F32), two, sds((2, 8, NY), F32)),
        [VMEM] * 8,
        (VMEM, VMEM, VMEM),
        name="outer_runs",
    )(first_tiles, last_tiles, nxt, prv, *inner)
    recv = lax.all_to_all(send, "tm", 0, 0)
    back, sums = call(
        functools.partial(sum_kernel, size),
        (sds((NW, 32, HALF), F32), sds((size, 1, HALF), F32)),
        [VMEM] * 2,
        (VMEM, VMEM),
        name="window_sums",
    )(recv, part)
    sums = lax.all_to_all(sums, "space", 0, 0)
    back = call(
        functools.partial(join_kernel, size),
        sds((NW, 40, HALF), F32),
        [VMEM] * 2,
        VMEM,
        name="join",
    )(sums, back)
    back = lax.all_to_all(back, "tm", 0, 0)
    return call(
        update_kernel,
        (sds(lag.shape, F32), sds(obs.shape, F32), sds(inc.shape, F32)),
        [VMEM] * 5,
        (VMEM, VMEM, VMEM),
        name="update",
    )(back, lag, obs, inc, zobs)


def solution(mesh):
    field = P("tm", None, "space", None)
    pair = P("tm", None, None, "space", None)
    coef = P(None, "space", None)
    return jax.shard_map(
        body,
        mesh=mesh,
        in_specs=(field, pair, field, field, pair, field, pair, coef, coef, coef),
        out_specs=(field, pair, field),
        check_vma=False,
    )
```

```python
import functools

import jax
import jax.numpy as jnp
from jax import lax
from jax.experimental import pallas as pl
from jax.experimental.pallas import tpu as pltpu
from jax.sharding import PartitionSpec as P

STEPS = 4
LEV = 4
ROWS = 32
NY = 256
NW = 16
HALF = 128
EDGE = 7
F32 = jnp.float32

VMEM = pl.BlockSpec(memory_space=pltpu.VMEM)
ANY = pl.BlockSpec(memory_space=pl.ANY)


def call(kernel, out_shape, in_specs, out_specs, scratch=(), **kw):
    return pl.pallas_call(
        kernel,
        out_shape=out_shape,
        in_specs=in_specs,
        out_specs=out_specs,
        scratch_shapes=list(scratch),
        compiler_params=pltpu.CompilerParams(vmem_limit_bytes=16 * 1024 * 1024),
        **kw,
    )


def edge_kernel(lag, obs, inc, cx, cy, df, first_out, last_out, first, last, sem):
    sources = [inc.at[0], obs.at[0, 1], obs.at[0, 0], lag.at[0], cx, cy, df]
    copies = []
    for f, src in enumerate(sources):
        copies.append(pltpu.make_async_copy(src.at[:, pl.ds(0, 8)], first.at[f], sem.at[2 * f]))
        copies.append(pltpu.make_async_copy(src.at[:, pl.ds(ROWS - 8, 8)], last.at[f], sem.at[2 * f + 1]))
    for c in copies:
        c.start()
    for c in copies:
        c.wait()
    low = lax.broadcasted_iota(jnp.int32, (8, NY), 0) < 4
    for f in range(EDGE):
        for m in range(2):
            k = 8 * (2 * f + m)
            first_out[k : k + 8, :] = jnp.where(low, first[f, 2 * m], pltpu.roll(first[f, 2 * m + 1], 4, 0))
            last_out[k : k + 8, :] = jnp.where(low, pltpu.roll(last[f, 2 * m], 4, 0), last[f, 2 * m + 1])


def turn(x, rows):
    return pltpu.roll(x, rows % x.shape[0], 0)


def north(x):
    return pltpu.roll(x, NY - 1, 1)


def south(x):
    return pltpu.roll(x, 1, 1)


def weights(cx, cy, df):
    col = lax.broadcasted_iota(jnp.int32, df.shape, 1)
    x, y = 0.5 * cx, 0.5 * cy
    an = jnp.where(col == NY - 1, 0.0, df - y)
    as_ = jnp.where(col == 0, 0.0, df + y)
    return 1.0 - 4.0 * df, df - x, df + x, an, as_


def along_y(p, c):
    return c[0] * p + north(c[4] * p) + south(c[3] * p)


def inner_kernel(lag, obs, inc, mside, oside, mvar, ovar, cx, cy, df, fixed, states, resid, inverse, feed):
    tile_row = lax.broadcasted_iota(jnp.int32, (8, NY), 0)
    row = lax.broadcasted_iota(jnp.int32, (ROWS, NY), 0)

    def hand_over(l, run, step, up, down):
        m, h = l // 2, 4 * (l % 2)
        for side, (x, at, to) in enumerate(((up, 7, h + step + 1), (down, 0, h + 2 - step))):
            other = 0.0 if h == 0 else feed[side, run, step, m]
            feed[side, run, step, m] = jnp.where(tile_row == to, turn(x, to - at), other)

    for l in range(LEV):
        a0, ae_full, aw_full, an, as_ = c = weights(cx[l], cy[l], df[l])
        ae = jnp.where(row == ROWS - 1, 0.0, ae_full)
        aw = jnp.where(row == 0, 0.0, aw_full)
        lagr = lag[0, l]
        q, p, b = inc[0, l], obs[0, 1, l], lagr
        for step in range(STEPS):
            if step == STEPS // 2:
                states[0, l] = q
                p = p + obs[0, 0, l]
            if step < STEPS - 1:
                hand_over(l, 0, step, q[ROWS - 8 :], q[:8])
                for run, x in ((1, p), (2, b)):
                    hand_over(l, run, step, ae_full[ROWS - 8 :] * x[ROWS - 8 :], aw_full[:8] * x[:8])
            q = a0 * q + ae * turn(q, -1) + aw * turn(q, 1) + an * north(q) + as_ * south(q)
            p = along_y(p, c) + turn(aw * p, -1) + turn(ae * p, 1)
            b = along_y(b, c) + turn(aw * b, -1) + turn(ae * b, 1)
        states[1, l] = q
        states[2, l] = p + lagr
        states[3, l] = b
        fixed[l] = mside[0, l] - mvar[0, l] * lagr - inc[0, l]
        for j in range(2):
            var = ovar[0, j, l]
            resid[j, l] = oside[0, j, l] - var * obs[0, j, l]
            inverse[j, l] = 1.0 / var


def added(side, m, first, last, nxt, prv, feed):
    i = lax.broadcasted_iota(jnp.int32, (8, NY), 0) & 3
    inward = 1 - 2 * side

    def tile(ref, f):
        k = 8 * (2 * f + m)
        return ref[k : k + 8, :]

    def rows(f, s):
        outer, inner = (nxt, last) if side == 0 else (prv, first)
        if s == 0:
            return tile(outer, f)
        if s == 4:
            return tile(inner, f)
        own = i < s if side == 0 else i >= 4 - s
        return jnp.where(own, turn(tile(inner, f), inward * (s - 4)), turn(tile(outer, f), inward * s))

    def moved(x, n):
        keep = i >= n if side == 0 else i < 4 - n
        return jnp.where(keep, turn(x, inward * n), 0.0)

    q, p, b = tile(nxt if side == 0 else prv, 0), rows(1, 0), rows(3, 0)
    here = weights(rows(4, 0), rows(5, 0), rows(6, 0))
    for s in range(STEPS):
        if s == STEPS // 2:
            middle = q
            p = p + moved(rows(2, 0), 2)
        there = weights(rows(4, s + 1), rows(5, s + 1), rows(6, s + 1))
        a0, ae, aw, an, as_ = there
        ahead, behind = (ae, aw) if side == 0 else (aw, ae)
        mid = moved(q, 1)
        past = moved(q, 2)
        if s < STEPS - 1:
            past = past + feed[side, 0, s, m]
        q = a0 * mid + ahead * q + behind * past + an * north(mid) + as_ * south(mid)
        ahead, behind = (here[2], here[1]) if side == 0 else (here[1], here[2])
        out = []
        for run, x in ((1, p), (2, b)):
            y = moved(along_y(x, here), 1) + ahead * x + moved(behind * x, 2)
            if s < STEPS - 1:
                y = y + feed[side, run, s, m]
            out.append(y)
        p, b = out
        here = there
    return middle, q, p, b


def outer_kernel(first, last, nxt, prv, fixed, states, resid, inverse, feed, send, zobs, part):
    row = lax.broadcasted_iota(jnp.int32, (8, NY), 0)
    cross = jnp.zeros((8, NY), F32)
    square = jnp.zeros((8, NY), F32)
    for m in range(2):
        more = [added(side, m, first, last, nxt, prv, feed) for side in range(2)]
        for h in range(2):
            l = 2 * m + h
            for k in range(4):
                rows = slice(8 * k, 8 * k + 8)
                tiles = [states[n, l, rows, :] for n in range(4)]
                if k == 0:
                    mid, *end = more[1]
                    tiles[0] = tiles[0] + jnp.where(row < 2, turn(mid, -2 - 4 * h), 0.0)
                    for n in range(3):
                        tiles[n + 1] = tiles[n + 1] + jnp.where(row < 4, turn(end[n], -4 * h), 0.0)
                if k == 3:
                    mid, *end = more[0]
                    tiles[0] = tiles[0] + jnp.where(row >= 6, turn(mid, 6 - 4 * h), 0.0)
                    for n in range(3):
                        tiles[n + 1] = tiles[n + 1] + jnp.where(row >= 4, turn(end[n], 4 - 4 * h), 0.0)
                t = 4 * l + k
                send[t, 0:8, :] = fixed[l, rows, :]
                for n in range(1, 4):
                    send[t, 8 * n : 8 * n + 8, :] = tiles[n]
                for j in range(2):
                    r = resid[j, l, rows, :] - tiles[j]
                    z = r * inverse[j, l, rows, :]
                    zobs[j, l, rows, :] = z
                    cross = cross + r * z
                    square = square + z * z
    part[0] = cross
    part[1] = square


def sum_kernel(count, recv, part, back, out):
    cross, square = part[0], part[1]
    z = jnp.zeros((8, NY), F32)
    before = jnp.zeros((8, NY), F32)
    for w in range(NW):
        r = recv[w, 0:8, :] + before
        before = recv[w, 8:16, :]
        z = z + r
        cross = cross + r * z
        square = square + z * z
        back[w, 0:8, :] = z[:, :HALF]
        back[w, 8:16, :] = z[:, HALF:]
    z = jnp.zeros((8, NY), F32)
    after = jnp.zeros((8, NY), F32)
    for w in reversed(range(NW)):
        r = after - recv[w, 16:24, :]
        after = recv[w, 24:32, :]
        z = z + r
        cross = cross + r * z
        square = square + z * z
        back[w, 16:24, :] = z[:, :HALF]
        back[w, 24:32, :] = z[:, HALF:]

    def fold(v):
        v = v[:, :HALF] + v[:, HALF:]
        return v + pltpu.roll(v, HALF // 2, 1)

    lane = lax.broadcasted_iota(jnp.int32, (8, HALF), 1)
    both = jnp.where(lane < HALF // 2, fold(cross), fold(square))
    row = jnp.sum(both, axis=0, keepdims=True)
    for s in range(count):
        out[s] = row


def join_kernel(count, sums, back, out):
    total = sums[0]
    for s in range(1, count):
        total = total + sums[s]
    tile = jnp.broadcast_to(total, (8, HALF))
    for w in range(NW):
        out[w, 0:32, :] = back[w]
        out[w, 32:40, :] = tile


def update_kernel(recv, lag, obs, inc, zobs, lag_out, obs_out, inc_out):
    total = recv[0, 32:33, :]
    for w in range(1, NW):
        total = total + recv[w, 32:33, :]
    lane = lax.broadcasted_iota(jnp.int32, (1, HALF), 1)
    cross = jnp.sum(jnp.where(lane < HALF // 2, total, 0.0), axis=1, keepdims=True)
    square = jnp.sum(jnp.where(lane < HALF // 2, 0.0, total), axis=1, keepdims=True)
    step = cross / (square + 1e-06)
    for l in range(LEV):
        for k in range(4):
            rows = slice(8 * k, 8 * k + 8)
            t = 4 * l + k
            for h in range(2):
                cols = slice(HALF * h, HALF * h + HALF)
                lag_out[0, l, rows, cols] = lag[0, l, rows, cols] + step * recv[t, 8 * h : 8 * h + 8, :]
                inc_out[0, l, rows, cols] = inc[0, l, rows, cols] + step * recv[t, 16 + 8 * h : 24 + 8 * h, :]
        for j in range(2):
            obs_out[0, j, l] = obs[0, j, l] + step * zobs[j, l]


def body(lag, obs, inc, mside, oside, mvar, ovar, cx, cy, df):
    sds = jax.ShapeDtypeStruct
    size = lax.axis_size("space")
    edge = sds((EDGE * LEV * 4, NY), F32)
    one, two, four = (sds(n + (LEV, ROWS, NY), F32) for n in ((), (2,), (4,)))
    feed = sds((2, 3, STEPS - 1, LEV // 2, 8, NY), F32)
    held = [pltpu.with_memory_space_constraint(x, pltpu.HBM) for x in (lag, obs, inc, mside, oside, mvar, ovar, cx, cy, df)]
    first, last = call(
        edge_kernel,
        (edge, edge),
        [ANY] * 6,
        (VMEM,) * 2,
        [pltpu.VMEM((EDGE, LEV, 8, NY), F32)] * 2 + [pltpu.SemaphoreType.DMA((2 * EDGE,))],
        name="edges",
    )(*held[:3], *held[7:])
    nxt = lax.ppermute(first, "space", [((i + 1) % size, i) for i in range(size)])
    prv = lax.ppermute(last, "space", [(i, (i + 1) % size) for i in range(size)])
    inner = call(
        inner_kernel,
        (one, four, two, two, feed),
        [VMEM] * 10,
        (VMEM,) * 5,
        name="inner_runs",
        cost_estimate=pl.CostEstimate(flops=8 * 1024 * 1024, bytes_accessed=4 * 1024 * 1024, transcendentals=0),
    )(*held)
    send, zobs, part = call(
        outer_kernel,
        (sds((NW, 32, NY), F32), two, sds((2, 8, NY), F32)),
        [VMEM] * 9,
        (VMEM, VMEM, VMEM),
        name="outer_runs",
    )(first, last, nxt, prv, *inner)
    recv = lax.all_to_all(send, "tm", 0, 0)
    back, sums = call(
        functools.partial(sum_kernel, size),
        (sds((NW, 32, HALF), F32), sds((size, 1, HALF), F32)),
        [VMEM] * 2,
        (VMEM, VMEM),
        name="window_sums",
    )(recv, part)
    sums = lax.all_to_all(sums, "space", 0, 0)
    back = call(
        functools.partial(join_kernel, size),
        sds((NW, 40, HALF), F32),
        [VMEM] * 2,
        VMEM,
        name="join",
    )(sums, back)
    back = lax.all_to_all(back, "tm", 0, 0)
    return call(
        update_kernel,
        (sds(lag.shape, F32), sds(obs.shape, F32), sds(inc.shape, F32)),
        [VMEM] * 5,
        (VMEM, VMEM, VMEM),
        name="update",
    )(back, lag, obs, inc, zobs)


def solution(mesh):
    field = P("tm", None, "space", None)
    pair = P("tm", None, None, "space", None)
    coef = P(None, "space", None)
    return jax.shard_map(
        body,
        mesh=mesh,
        in_specs=(field, pair, field, field, pair, field, pair, coef, coef, coef),
        out_specs=(field, pair, field),
        check_vma=False,
    )
```

```python
import functools

import jax
import jax.numpy as jnp
from jax import lax
from jax.experimental import pallas as pl
from jax.experimental.pallas import tpu as pltpu
from jax.sharding import PartitionSpec as P

STEPS = 4
LEV = 4
ROWS = 32
NY = 256
NW = 16
HALF = 128
EDGE = 7
F32 = jnp.float32

SPACE_ORDER = [2 * (z % 16) + core for z in range(26, 10, -1) for core in (1, 0)]
OUT_ORDER = [10, 6, 9, 11, 14, 2, 5, 7, 8, 13, 15, 1, 3, 4, 12, 0]
BACK_ORDER = OUT_ORDER
OUT_AT = [OUT_ORDER.index(w) for w in range(NW)]
BACK_AT = [BACK_ORDER.index(w) for w in range(NW)]

VMEM = pl.BlockSpec(memory_space=pltpu.VMEM)
ANY = pl.BlockSpec(memory_space=pl.ANY)


def call(kernel, out_shape, in_specs, out_specs, scratch=(), **kw):
    return pl.pallas_call(
        kernel,
        out_shape=out_shape,
        in_specs=in_specs,
        out_specs=out_specs,
        scratch_shapes=list(scratch),
        compiler_params=pltpu.CompilerParams(vmem_limit_bytes=16 * 1024 * 1024),
        **kw,
    )


def edge_kernel(lag, obs, inc, cx, cy, df, first_out, last_out, first, last, sem):
    sources = [inc.at[0], obs.at[0, 1], obs.at[0, 0], lag.at[0], cx, cy, df]
    copies = []
    for f, src in enumerate(sources):
        copies.append(pltpu.make_async_copy(src.at[:, pl.ds(0, 8)], first.at[f], sem.at[2 * f]))
        copies.append(pltpu.make_async_copy(src.at[:, pl.ds(ROWS - 8, 8)], last.at[f], sem.at[2 * f + 1]))
    for c in copies:
        c.start()
    for c in copies:
        c.wait()
    low = lax.broadcasted_iota(jnp.int32, (8, NY), 0) < 4
    for f in range(EDGE):
        for m in range(2):
            k = 8 * (2 * f + m)
            first_out[k : k + 8, :] = jnp.where(low, first[f, 2 * m], pltpu.roll(first[f, 2 * m + 1], 4, 0))
            last_out[k : k + 8, :] = jnp.where(low, pltpu.roll(last[f, 2 * m], 4, 0), last[f, 2 * m + 1])


def turn(x, rows):
    return pltpu.roll(x, rows % x.shape[0], 0)


def north(x):
    return pltpu.roll(x, NY - 1, 1)


def south(x):
    return pltpu.roll(x, 1, 1)


def weights(cx, cy, df):
    col = lax.broadcasted_iota(jnp.int32, df.shape, 1)
    x, y = 0.5 * cx, 0.5 * cy
    an = jnp.where(col == NY - 1, 0.0, df - y)
    as_ = jnp.where(col == 0, 0.0, df + y)
    return 1.0 - 4.0 * df, df - x, df + x, an, as_


def along_y(p, c):
    return c[0] * p + north(c[4] * p) + south(c[3] * p)


def inner_kernel(lag, obs, inc, mside, oside, mvar, ovar, cx, cy, df, fixed, states, resid, inverse, feed):
    tile_row = lax.broadcasted_iota(jnp.int32, (8, NY), 0)
    row = lax.broadcasted_iota(jnp.int32, (ROWS, NY), 0)

    def hand_over(l, run, step, up, down):
        m, h = l // 2, 4 * (l % 2)
        for side, (x, at, to) in enumerate(((up, 7, h + step + 1), (down, 0, h + 2 - step))):
            other = 0.0 if h == 0 else feed[side, run, step, m]
            feed[side, run, step, m] = jnp.where(tile_row == to, turn(x, to - at), other)

    for l in range(LEV):
        a0, ae_full, aw_full, an, as_ = c = weights(cx[l], cy[l], df[l])
        ae = jnp.where(row == ROWS - 1, 0.0, ae_full)
        aw = jnp.where(row == 0, 0.0, aw_full)
        lagr = lag[0, l]
        q, p, b = inc[0, l], obs[0, 1, l], lagr
        for step in range(STEPS):
            if step == STEPS // 2:
                states[0, l] = q
                p = p + obs[0, 0, l]
            if step < STEPS - 1:
                hand_over(l, 0, step, q[ROWS - 8 :], q[:8])
                for run, x in ((1, p), (2, b)):
                    hand_over(l, run, step, ae_full[ROWS - 8 :] * x[ROWS - 8 :], aw_full[:8] * x[:8])
            q = a0 * q + ae * turn(q, -1) + aw * turn(q, 1) + an * north(q) + as_ * south(q)
            p = along_y(p, c) + turn(aw * p, -1) + turn(ae * p, 1)
            b = along_y(b, c) + turn(aw * b, -1) + turn(ae * b, 1)
        states[1, l] = q
        states[2, l] = p + lagr
        states[3, l] = b
        fixed[l] = mside[0, l] - mvar[0, l] * lagr - inc[0, l]
        for j in range(2):
            var = ovar[0, j, l]
            resid[j, l] = oside[0, j, l] - var * obs[0, j, l]
            inverse[j, l] = 1.0 / var


def added(side, m, first, last, nxt, prv, feed):
    i = lax.broadcasted_iota(jnp.int32, (8, NY), 0) & 3
    inward = 1 - 2 * side

    def tile(ref, f):
        k = 8 * (2 * f + m)
        return ref[k : k + 8, :]

    def rows(f, s):
        outer, inner = (nxt, last) if side == 0 else (prv, first)
        if s == 0:
            return tile(outer, f)
        if s == 4:
            return tile(inner, f)
        own = i < s if side == 0 else i >= 4 - s
        return jnp.where(own, turn(tile(inner, f), inward * (s - 4)), turn(tile(outer, f), inward * s))

    def moved(x, n):
        keep = i >= n if side == 0 else i < 4 - n
        return jnp.where(keep, turn(x, inward * n), 0.0)

    q, p, b = tile(nxt if side == 0 else prv, 0), rows(1, 0), rows(3, 0)
    here = weights(rows(4, 0), rows(5, 0), rows(6, 0))
    for s in range(STEPS):
        if s == STEPS // 2:
            middle = q
            p = p + moved(rows(2, 0), 2)
        there = weights(rows(4, s + 1), rows(5, s + 1), rows(6, s + 1))
        a0, ae, aw, an, as_ = there
        ahead, behind = (ae, aw) if side == 0 else (aw, ae)
        mid = moved(q, 1)
        past = moved(q, 2)
        if s < STEPS - 1:
            past = past + feed[side, 0, s, m]
        q = a0 * mid + ahead * q + behind * past + an * north(mid) + as_ * south(mid)
        ahead, behind = (here[2], here[1]) if side == 0 else (here[1], here[2])
        out = []
        for run, x in ((1, p), (2, b)):
            y = moved(along_y(x, here), 1) + ahead * x + moved(behind * x, 2)
            if s < STEPS - 1:
                y = y + feed[side, run, s, m]
            out.append(y)
        p, b = out
        here = there
    return middle, q, p, b


def outer_kernel(first, last, nxt, prv, fixed, states, resid, inverse, feed, send, zobs, part):
    row = lax.broadcasted_iota(jnp.int32, (8, NY), 0)
    cross = jnp.zeros((8, NY), F32)
    square = jnp.zeros((8, NY), F32)
    for m in range(2):
        more = [added(side, m, first, last, nxt, prv, feed) for side in range(2)]
        for h in range(2):
            l = 2 * m + h
            for k in range(4):
                rows = slice(8 * k, 8 * k + 8)
                tiles = [states[n, l, rows, :] for n in range(4)]
                if k == 0:
                    mid, *end = more[1]
                    tiles[0] = tiles[0] + jnp.where(row < 2, turn(mid, -2 - 4 * h), 0.0)
                    for n in range(3):
                        tiles[n + 1] = tiles[n + 1] + jnp.where(row < 4, turn(end[n], -4 * h), 0.0)
                if k == 3:
                    mid, *end = more[0]
                    tiles[0] = tiles[0] + jnp.where(row >= 6, turn(mid, 6 - 4 * h), 0.0)
                    for n in range(3):
                        tiles[n + 1] = tiles[n + 1] + jnp.where(row >= 4, turn(end[n], 4 - 4 * h), 0.0)
                t = OUT_AT[4 * l + k]
                send[t, 0:8, :] = fixed[l, rows, :]
                for n in range(1, 4):
                    send[t, 8 * n : 8 * n + 8, :] = tiles[n]
                for j in range(2):
                    r = resid[j, l, rows, :] - tiles[j]
                    z = r * inverse[j, l, rows, :]
                    zobs[j, l, rows, :] = z
                    cross = cross + r * z
                    square = square + z * z
    part[0] = cross
    part[1] = square


def sum_kernel(count, recv, part, back, out):
    cross, square = part[0], part[1]
    z = jnp.zeros((8, NY), F32)
    before = jnp.zeros((8, NY), F32)
    for w in range(NW):
        i, o = OUT_AT[w], BACK_AT[w]
        r = recv[i, 0:8, :] + before
        before = recv[i, 8:16, :]
        z = z + r
        cross = cross + r * z
        square = square + z * z
        back[o, 0:8, :] = z[:, :HALF]
        back[o, 8:16, :] = z[:, HALF:]
    z = jnp.zeros((8, NY), F32)
    after = jnp.zeros((8, NY), F32)
    for w in reversed(range(NW)):
        i, o = OUT_AT[w], BACK_AT[w]
        r = after - recv[i, 16:24, :]
        after = recv[i, 24:32, :]
        z = z + r
        cross = cross + r * z
        square = square + z * z
        back[o, 16:24, :] = z[:, :HALF]
        back[o, 24:32, :] = z[:, HALF:]

    def fold(v):
        v = v[:, :HALF] + v[:, HALF:]
        return v + pltpu.roll(v, HALF // 2, 1)

    lane = lax.broadcasted_iota(jnp.int32, (8, HALF), 1)
    both = jnp.where(lane < HALF // 2, fold(cross), fold(square))
    row = jnp.sum(both, axis=0, keepdims=True)
    for s in range(count):
        out[s] = row


def join_kernel(count, sums, back, out):
    total = sums[0]
    for s in range(1, count):
        total = total + sums[s]
    tile = jnp.broadcast_to(total, (8, HALF))
    for w in range(NW):
        out[w, 0:32, :] = back[w]
        out[w, 32:40, :] = tile


def update_kernel(recv, lag, obs, inc, zobs, lag_out, obs_out, inc_out):
    total = recv[0, 32:33, :]
    for w in range(1, NW):
        total = total + recv[w, 32:33, :]
    lane = lax.broadcasted_iota(jnp.int32, (1, HALF), 1)
    cross = jnp.sum(jnp.where(lane < HALF // 2, total, 0.0), axis=1, keepdims=True)
    square = jnp.sum(jnp.where(lane < HALF // 2, 0.0, total), axis=1, keepdims=True)
    step = cross / (square + 1e-06)
    for l in range(LEV):
        for k in range(4):
            rows = slice(8 * k, 8 * k + 8)
            t = BACK_AT[4 * l + k]
            for h in range(2):
                cols = slice(HALF * h, HALF * h + HALF)
                lag_out[0, l, rows, cols] = lag[0, l, rows, cols] + step * recv[t, 8 * h : 8 * h + 8, :]
                inc_out[0, l, rows, cols] = inc[0, l, rows, cols] + step * recv[t, 16 + 8 * h : 24 + 8 * h, :]
        for j in range(2):
            obs_out[0, j, l] = obs[0, j, l] + step * zobs[j, l]


def body(lag, obs, inc, mside, oside, mvar, ovar, cx, cy, df):
    sds = jax.ShapeDtypeStruct
    size = lax.axis_size("space")
    edge = sds((EDGE * LEV * 4, NY), F32)
    one, two, four = (sds(n + (LEV, ROWS, NY), F32) for n in ((), (2,), (4,)))
    feed = sds((2, 3, STEPS - 1, LEV // 2, 8, NY), F32)
    held = [pltpu.with_memory_space_constraint(x, pltpu.HBM) for x in (lag, obs, inc, mside, oside, mvar, ovar, cx, cy, df)]
    first, last = call(
        edge_kernel,
        (edge, edge),
        [ANY] * 6,
        (VMEM,) * 2,
        [pltpu.VMEM((EDGE, LEV, 8, NY), F32)] * 2 + [pltpu.SemaphoreType.DMA((2 * EDGE,))],
        name="edges",
    )(*held[:3], *held[7:])
    nxt = lax.ppermute(first, "space", [((i + 1) % size, i) for i in range(size)])
    prv = lax.ppermute(last, "space", [(i, (i + 1) % size) for i in range(size)])
    inner = call(
        inner_kernel,
        (one, four, two, two, feed),
        [VMEM] * 10,
        (VMEM,) * 5,
        name="inner_runs",
        cost_estimate=pl.CostEstimate(flops=8 * 1024 * 1024, bytes_accessed=4 * 1024 * 1024, transcendentals=0),
    )(*held)
    send, zobs, part = call(
        outer_kernel,
        (sds((NW, 32, NY), F32), two, sds((2, 8, NY), F32)),
        [VMEM] * 9,
        (VMEM, VMEM, VMEM),
        name="outer_runs",
    )(first, last, nxt, prv, *inner)
    recv = lax.all_to_all(send, "tm", 0, 0, axis_index_groups=[OUT_ORDER])
    back, sums = call(
        functools.partial(sum_kernel, size),
        (sds((NW, 32, HALF), F32), sds((size, 1, HALF), F32)),
        [VMEM] * 2,
        (VMEM, VMEM),
        name="window_sums",
    )(recv, part)
    sums = lax.all_to_all(sums, "space", 0, 0, axis_index_groups=[SPACE_ORDER])
    back = call(
        functools.partial(join_kernel, size),
        sds((NW, 40, HALF), F32),
        [VMEM] * 2,
        VMEM,
        name="join",
    )(sums, back)
    back = lax.all_to_all(back, "tm", 0, 0, axis_index_groups=[BACK_ORDER])
    return call(
        update_kernel,
        (sds(lag.shape, F32), sds(obs.shape, F32), sds(inc.shape, F32)),
        [VMEM] * 5,
        (VMEM, VMEM, VMEM),
        name="update",
    )(back, lag, obs, inc, zobs)


def solution(mesh):
    field = P("tm", None, "space", None)
    pair = P("tm", None, None, "space", None)
    coef = P(None, "space", None)
    return jax.shard_map(
        body,
        mesh=mesh,
        in_specs=(field, pair, field, field, pair, field, pair, coef, coef, coef),
        out_specs=(field, pair, field),
        check_vma=False,
    )
```

```python
import functools

import jax
import jax.numpy as jnp
from jax import lax
from jax.experimental import pallas as pl
from jax.experimental.pallas import tpu as pltpu
from jax.sharding import PartitionSpec as P

STEPS = 4
LEV = 4
ROWS = 32
NY = 256
NW = 16
HALF = 128
EDGE = 7
F32 = jnp.float32

SPACE_ORDER = [2 * (z % 16) + core for z in range(26, 10, -1) for core in (1, 0)]
OUT_ORDER = [10, 6, 9, 11, 14, 2, 5, 7, 8, 13, 15, 1, 3, 4, 12, 0]
BACK_ORDER = OUT_ORDER
OUT_AT = [OUT_ORDER.index(w) for w in range(NW)]
BACK_AT = [BACK_ORDER.index(w) for w in range(NW)]

VMEM = pl.BlockSpec(memory_space=pltpu.VMEM)
ANY = pl.BlockSpec(memory_space=pl.ANY)


def call(kernel, out_shape, in_specs, out_specs, scratch=(), **kw):
    return pl.pallas_call(
        kernel,
        out_shape=out_shape,
        in_specs=in_specs,
        out_specs=out_specs,
        scratch_shapes=list(scratch),
        compiler_params=pltpu.CompilerParams(vmem_limit_bytes=16 * 1024 * 1024),
        **kw,
    )


def tile_of(f, m):
    return 8 * (2 * f + m if f < 2 else 4 if f == 2 else 2 * f + m - 1)


def edge_kernel(lag, obs, inc, cx, cy, df, first_out, last_out, first, last, sem):
    sources = [inc.at[0], obs.at[0, 1], obs.at[0, 0], lag.at[0], cx, cy, df]
    copies = []
    for f, src in enumerate(sources):
        copies.append(pltpu.make_async_copy(src.at[:, pl.ds(0, 8)], first.at[f], sem.at[2 * f]))
        copies.append(pltpu.make_async_copy(src.at[:, pl.ds(ROWS - 8, 8)], last.at[f], sem.at[2 * f + 1]))
    for c in copies:
        c.start()
    for c in copies:
        c.wait()
    row = lax.broadcasted_iota(jnp.int32, (8, NY), 0)
    low = row < 4
    two_first = two_last = jnp.zeros((8, NY), F32)
    for l in range(LEV):
        at = 4 * (l % 2) + 2 * (l // 2)
        mine = (row >= at) & (row < at + 2)
        two_first = jnp.where(mine, turn(first[2, l], at), two_first)
        two_last = jnp.where(mine, turn(last[2, l], at - 6), two_last)
    k = tile_of(2, 0)
    first_out[k : k + 8, :] = two_first
    last_out[k : k + 8, :] = two_last
    for f in (0, 1, 3, 4, 5, 6):
        for m in range(2):
            k = tile_of(f, m)
            first_out[k : k + 8, :] = jnp.where(low, first[f, 2 * m], pltpu.roll(first[f, 2 * m + 1], 4, 0))
            last_out[k : k + 8, :] = jnp.where(low, pltpu.roll(last[f, 2 * m], 4, 0), last[f, 2 * m + 1])


def turn(x, rows):
    return pltpu.roll(x, rows % x.shape[0], 0)


def north(x):
    return pltpu.roll(x, NY - 1, 1)


def south(x):
    return pltpu.roll(x, 1, 1)


def weights(cx, cy, df):
    col = lax.broadcasted_iota(jnp.int32, df.shape, 1)
    x, y = 0.5 * cx, 0.5 * cy
    an = jnp.where(col == NY - 1, 0.0, df - y)
    as_ = jnp.where(col == 0, 0.0, df + y)
    return 1.0 - 4.0 * df, df - x, df + x, an, as_


def along_y(p, c):
    return c[0] * p + north(c[4] * p) + south(c[3] * p)


def inner_kernel(lag, obs, inc, mside, oside, mvar, ovar, cx, cy, df, fixed, states, resid, inverse, feed):
    tile_row = lax.broadcasted_iota(jnp.int32, (8, NY), 0)
    row = lax.broadcasted_iota(jnp.int32, (ROWS, NY), 0)

    def hand_over(l, run, step, up, down):
        m, h = l // 2, 4 * (l % 2)
        for side, (x, at, to) in enumerate(((up, 7, h + step + 1), (down, 0, h + 2 - step))):
            other = 0.0 if h == 0 else feed[side, run, step, m]
            feed[side, run, step, m] = jnp.where(tile_row == to, turn(x, to - at), other)

    for l in range(LEV):
        a0, ae_full, aw_full, an, as_ = c = weights(cx[l], cy[l], df[l])
        ae = jnp.where(row == ROWS - 1, 0.0, ae_full)
        aw = jnp.where(row == 0, 0.0, aw_full)
        lagr = lag[0, l]
        q, p, b = inc[0, l], obs[0, 1, l], lagr
        for step in range(STEPS):
            if step == STEPS // 2:
                states[0, l] = q
                p = p + obs[0, 0, l]
            if step < STEPS - 1:
                hand_over(l, 0, step, q[ROWS - 8 :], q[:8])
                for run, x in ((1, p), (2, b)):
                    hand_over(l, run, step, ae_full[ROWS - 8 :] * x[ROWS - 8 :], aw_full[:8] * x[:8])
            q = a0 * q + ae * turn(q, -1) + aw * turn(q, 1) + an * north(q) + as_ * south(q)
            p = along_y(p, c) + turn(aw * p, -1) + turn(ae * p, 1)
            b = along_y(b, c) + turn(aw * b, -1) + turn(ae * b, 1)
        states[1, l] = q
        states[2, l] = p + lagr
        states[3, l] = b
        fixed[l] = mside[0, l] - mvar[0, l] * lagr - inc[0, l]
        for j in range(2):
            var = ovar[0, j, l]
            resid[j, l] = oside[0, j, l] - var * obs[0, j, l]
            inverse[j, l] = 1.0 / var


def added(side, m, first, last, nxt, prv, feed):
    i = lax.broadcasted_iota(jnp.int32, (8, NY), 0) & 3
    inward = 1 - 2 * side

    def tile(ref, f):
        k = tile_of(f, m)
        return ref[k : k + 8, :]

    def rows(f, s):
        outer, inner = (nxt, last) if side == 0 else (prv, first)
        if s == 0:
            return tile(outer, f)
        if s == 4:
            return tile(inner, f)
        own = i < s if side == 0 else i >= 4 - s
        return jnp.where(own, turn(tile(inner, f), inward * (s - 4)), turn(tile(outer, f), inward * s))

    def moved(x, n):
        keep = i >= n if side == 0 else i < 4 - n
        return jnp.where(keep, turn(x, inward * n), 0.0)

    q, p, b = tile(nxt if side == 0 else prv, 0), rows(1, 0), rows(3, 0)
    here = weights(rows(4, 0), rows(5, 0), rows(6, 0))
    for s in range(STEPS):
        if s == STEPS // 2:
            middle = q
            force = tile(nxt if side == 0 else prv, 2)
            force = turn(force, 2 - 2 * m if side == 0 else -2 * m)
            p = p + jnp.where(i >= 2 if side == 0 else i < 2, force, 0.0)
        there = weights(rows(4, s + 1), rows(5, s + 1), rows(6, s + 1))
        a0, ae, aw, an, as_ = there
        ahead, behind = (ae, aw) if side == 0 else (aw, ae)
        mid = moved(q, 1)
        past = moved(q, 2)
        if s < STEPS - 1:
            past = past + feed[side, 0, s, m]
        q = a0 * mid + ahead * q + behind * past + an * north(mid) + as_ * south(mid)
        ahead, behind = (here[2], here[1]) if side == 0 else (here[1], here[2])
        out = []
        for run, x in ((1, p), (2, b)):
            y = moved(along_y(x, here), 1) + ahead * x + moved(behind * x, 2)
            if s < STEPS - 1:
                y = y + feed[side, run, s, m]
            out.append(y)
        p, b = out
        here = there
    return middle, q, p, b


def outer_kernel(first, last, nxt, prv, fixed, states, resid, inverse, feed, send, zobs, part):
    row = lax.broadcasted_iota(jnp.int32, (8, NY), 0)
    cross = jnp.zeros((8, NY), F32)
    square = jnp.zeros((8, NY), F32)
    for m in range(2):
        more = [added(side, m, first, last, nxt, prv, feed) for side in range(2)]
        for h in range(2):
            l = 2 * m + h
            for k in range(4):
                rows = slice(8 * k, 8 * k + 8)
                tiles = [states[n, l, rows, :] for n in range(4)]
                if k == 0:
                    mid, *end = more[1]
                    tiles[0] = tiles[0] + jnp.where(row < 2, turn(mid, -2 - 4 * h), 0.0)
                    for n in range(3):
                        tiles[n + 1] = tiles[n + 1] + jnp.where(row < 4, turn(end[n], -4 * h), 0.0)
                if k == 3:
                    mid, *end = more[0]
                    tiles[0] = tiles[0] + jnp.where(row >= 6, turn(mid, 6 - 4 * h), 0.0)
                    for n in range(3):
                        tiles[n + 1] = tiles[n + 1] + jnp.where(row >= 4, turn(end[n], 4 - 4 * h), 0.0)
                t = OUT_AT[4 * l + k]
                send[t, 0:8, :] = fixed[l, rows, :]
                for n in range(1, 4):
                    send[t, 8 * n : 8 * n + 8, :] = tiles[n]
                for j in range(2):
                    r = resid[j, l, rows, :] - tiles[j]
                    z = r * inverse[j, l, rows, :]
                    zobs[j, l, rows, :] = z
                    cross = cross + r * z
                    square = square + z * z
    part[0] = cross
    part[1] = square


def sum_kernel(count, recv, part, back, out):
    cross, square = part[0], part[1]
    z = jnp.zeros((8, NY), F32)
    before = jnp.zeros((8, NY), F32)
    for w in range(NW):
        i, o = OUT_AT[w], BACK_AT[w]
        r = recv[i, 0:8, :] + before
        before = recv[i, 8:16, :]
        z = z + r
        cross = cross + r * z
        square = square + z * z
        back[o, 0:8, :] = z[:, :HALF]
        back[o, 8:16, :] = z[:, HALF:]
    z = jnp.zeros((8, NY), F32)
    after = jnp.zeros((8, NY), F32)
    for w in reversed(range(NW)):
        i, o = OUT_AT[w], BACK_AT[w]
        r = after - recv[i, 16:24, :]
        after = recv[i, 24:32, :]
        z = z + r
        cross = cross + r * z
        square = square + z * z
        back[o, 16:24, :] = z[:, :HALF]
        back[o, 24:32, :] = z[:, HALF:]

    def fold(v):
        v = v[:, :HALF] + v[:, HALF:]
        return v + pltpu.roll(v, HALF // 2, 1)

    lane = lax.broadcasted_iota(jnp.int32, (8, HALF), 1)
    both = jnp.where(lane < HALF // 2, fold(cross), fold(square))
    row = jnp.sum(both, axis=0, keepdims=True)
    for s in range(count):
        out[s] = row


def join_kernel(count, sums, back, out):
    total = sums[0]
    for s in range(1, count):
        total = total + sums[s]
    tile = jnp.broadcast_to(total, (8, HALF))
    for w in range(NW):
        out[w, 0:32, :] = back[w]
        out[w, 32:40, :] = tile


def update_kernel(recv, lag, obs, inc, zobs, lag_out, obs_out, inc_out):
    total = recv[0, 32:33, :]
    for w in range(1, NW):
        total = total + recv[w, 32:33, :]
    lane = lax.broadcasted_iota(jnp.int32, (1, HALF), 1)
    cross = jnp.sum(jnp.where(lane < HALF // 2, total, 0.0), axis=1, keepdims=True)
    square = jnp.sum(jnp.where(lane < HALF // 2, 0.0, total), axis=1, keepdims=True)
    step = cross / (square + 1e-06)
    for l in range(LEV):
        for k in range(4):
            rows = slice(8 * k, 8 * k + 8)
            t = BACK_AT[4 * l + k]
            for h in range(2):
                cols = slice(HALF * h, HALF * h + HALF)
                lag_out[0, l, rows, cols] = lag[0, l, rows, cols] + step * recv[t, 8 * h : 8 * h + 8, :]
                inc_out[0, l, rows, cols] = inc[0, l, rows, cols] + step * recv[t, 16 + 8 * h : 24 + 8 * h, :]
        for j in range(2):
            obs_out[0, j, l] = obs[0, j, l] + step * zobs[j, l]


def body(lag, obs, inc, mside, oside, mvar, ovar, cx, cy, df):
    sds = jax.ShapeDtypeStruct
    size = lax.axis_size("space")
    edge = sds((tile_of(EDGE, 0), NY), F32)
    one, two, four = (sds(n + (LEV, ROWS, NY), F32) for n in ((), (2,), (4,)))
    feed = sds((2, 3, STEPS - 1, LEV // 2, 8, NY), F32)
    held = [pltpu.with_memory_space_constraint(x, pltpu.HBM) for x in (lag, obs, inc, mside, oside, mvar, ovar, cx, cy, df)]
    first, last = call(
        edge_kernel,
        (edge, edge),
        [ANY] * 6,
        (VMEM,) * 2,
        [pltpu.VMEM((EDGE, LEV, 8, NY), F32)] * 2 + [pltpu.SemaphoreType.DMA((2 * EDGE,))],
        name="edges",
    )(*held[:3], *held[7:])
    nxt = lax.ppermute(first, "space", [((i + 1) % size, i) for i in range(size)])
    prv = lax.ppermute(last, "space", [(i, (i + 1) % size) for i in range(size)])
    inner = call(
        inner_kernel,
        (one, four, two, two, feed),
        [VMEM] * 10,
        (VMEM,) * 5,
        name="inner_runs",
        cost_estimate=pl.CostEstimate(flops=8 * 1024 * 1024, bytes_accessed=4 * 1024 * 1024, transcendentals=0),
    )(*held)
    send, zobs, part = call(
        outer_kernel,
        (sds((NW, 32, NY), F32), two, sds((2, 8, NY), F32)),
        [VMEM] * 9,
        (VMEM, VMEM, VMEM),
        name="outer_runs",
    )(first, last, nxt, prv, *inner)
    recv = lax.all_to_all(send, "tm", 0, 0, axis_index_groups=[OUT_ORDER])
    back, sums = call(
        functools.partial(sum_kernel, size),
        (sds((NW, 32, HALF), F32), sds((size, 1, HALF), F32)),
        [VMEM] * 2,
        (VMEM, VMEM),
        name="window_sums",
    )(recv, part)
    sums = lax.all_to_all(sums, "space", 0, 0, axis_index_groups=[SPACE_ORDER])
    back = call(
        functools.partial(join_kernel, size),
        sds((NW, 40, HALF), F32),
        [VMEM] * 2,
        VMEM,
        name="join",
    )(sums, back)
    back = lax.all_to_all(back, "tm", 0, 0, axis_index_groups=[BACK_ORDER])
    return call(
        update_kernel,
        (sds(lag.shape, F32), sds(obs.shape, F32), sds(inc.shape, F32)),
        [VMEM] * 5,
        (VMEM, VMEM, VMEM),
        name="update",
    )(back, lag, obs, inc, zobs)


def solution(mesh):
    field = P("tm", None, "space", None)
    pair = P("tm", None, None, "space", None)
    coef = P(None, "space", None)
    return jax.shard_map(
        body,
        mesh=mesh,
        in_specs=(field, pair, field, field, pair, field, pair, coef, coef, coef),
        out_specs=(field, pair, field),
        check_vma=False,
    )
```

```python
import functools

import jax
import jax.numpy as jnp
from jax import lax
from jax.experimental import pallas as pl
from jax.experimental.pallas import tpu as pltpu
from jax.sharding import PartitionSpec as P

STEPS = 4
LEV = 4
ROWS = 32
NY = 256
NW = 16
HALF = 128
EDGE = 7
F32 = jnp.float32

SPACE_ORDER = [2 * (z % 16) + core for z in range(26, 10, -1) for core in (1, 0)]
OUT_ORDER = [10, 6, 9, 11, 14, 2, 5, 7, 8, 13, 15, 1, 3, 4, 12, 0]
BACK_ORDER = OUT_ORDER[:1] + OUT_ORDER[:0:-1]
OUT_AT = [OUT_ORDER.index(w) for w in range(NW)]
BACK_AT = [BACK_ORDER.index(w) for w in range(NW)]

VMEM = pl.BlockSpec(memory_space=pltpu.VMEM)
ANY = pl.BlockSpec(memory_space=pl.ANY)


def call(kernel, out_shape, in_specs, out_specs, scratch=(), **kw):
    return pl.pallas_call(
        kernel,
        out_shape=out_shape,
        in_specs=in_specs,
        out_specs=out_specs,
        scratch_shapes=list(scratch),
        compiler_params=pltpu.CompilerParams(vmem_limit_bytes=16 * 1024 * 1024),
        **kw,
    )


def edge_kernel(lag, obs, inc, cx, cy, df, first_out, last_out, first, last, sem):
    sources = [inc.at[0], obs.at[0, 1], obs.at[0, 0], lag.at[0], cx, cy, df]
    copies = []
    for f, src in enumerate(sources):
        copies.append(pltpu.make_async_copy(src.at[:, pl.ds(0, 8)], first.at[f], sem.at[2 * f]))
        copies.append(pltpu.make_async_copy(src.at[:, pl.ds(ROWS - 8, 8)], last.at[f], sem.at[2 * f + 1]))
    for c in copies:
        c.start()
    for c in copies:
        c.wait()
    low = lax.broadcasted_iota(jnp.int32, (8, NY), 0) < 4
    for f in range(EDGE):
        for m in range(2):
            k = 8 * (2 * f + m)
            first_out[k : k + 8, :] = jnp.where(low, first[f, 2 * m], pltpu.roll(first[f, 2 * m + 1], 4, 0))
            last_out[k : k + 8, :] = jnp.where(low, pltpu.roll(last[f, 2 * m], 4, 0), last[f, 2 * m + 1])


def turn(x, rows):
    return pltpu.roll(x, rows % x.shape[0], 0)


def north(x):
    return pltpu.roll(x, NY - 1, 1)


def south(x):
    return pltpu.roll(x, 1, 1)


def weights(cx, cy, df):
    col = lax.broadcasted_iota(jnp.int32, df.shape, 1)
    x, y = 0.5 * cx, 0.5 * cy
    an = jnp.where(col == NY - 1, 0.0, df - y)
    as_ = jnp.where(col == 0, 0.0, df + y)
    return 1.0 - 4.0 * df, df - x, df + x, an, as_


def along_y(p, c):
    return c[0] * p + north(c[4] * p) + south(c[3] * p)


def inner_kernel(lag, obs, inc, mside, oside, mvar, ovar, cx, cy, df, fixed, states, resid, inverse, feed):
    tile_row = lax.broadcasted_iota(jnp.int32, (8, NY), 0)
    row = lax.broadcasted_iota(jnp.int32, (ROWS, NY), 0)

    def hand_over(l, run, step, up, down):
        m, h = l // 2, 4 * (l % 2)
        for side, (x, at, to) in enumerate(((up, 7, h + step + 1), (down, 0, h + 2 - step))):
            other = 0.0 if h == 0 else feed[side, run, step, m]
            feed[side, run, step, m] = jnp.where(tile_row == to, turn(x, to - at), other)

    for l in range(LEV):
        a0, ae_full, aw_full, an, as_ = c = weights(cx[l], cy[l], df[l])
        ae = jnp.where(row == ROWS - 1, 0.0, ae_full)
        aw = jnp.where(row == 0, 0.0, aw_full)
        lagr = lag[0, l]
        q, p, b = inc[0, l], obs[0, 1, l], lagr
        for step in range(STEPS):
            if step == STEPS // 2:
                states[0, l] = q
                p = p + obs[0, 0, l]
            if step < STEPS - 1:
                hand_over(l, 0, step, q[ROWS - 8 :], q[:8])
                for run, x in ((1, p), (2, b)):
                    hand_over(l, run, step, ae_full[ROWS - 8 :] * x[ROWS - 8 :], aw_full[:8] * x[:8])
            q = a0 * q + ae * turn(q, -1) + aw * turn(q, 1) + an * north(q) + as_ * south(q)
            p = along_y(p, c) + turn(aw * p, -1) + turn(ae * p, 1)
            b = along_y(b, c) + turn(aw * b, -1) + turn(ae * b, 1)
        states[1, l] = q
        states[2, l] = p + lagr
        states[3, l] = b
        fixed[l] = mside[0, l] - mvar[0, l] * lagr - inc[0, l]
        for j in range(2):
            var = ovar[0, j, l]
            resid[j, l] = oside[0, j, l] - var * obs[0, j, l]
            inverse[j, l] = 1.0 / var


def added(side, m, first, last, nxt, prv, feed):
    i = lax.broadcasted_iota(jnp.int32, (8, NY), 0) & 3
    inward = 1 - 2 * side

    def tile(ref, f):
        k = 8 * (2 * f + m)
        return ref[k : k + 8, :]

    def rows(f, s):
        outer, inner = (nxt, last) if side == 0 else (prv, first)
        if s == 0:
            return tile(outer, f)
        if s == 4:
            return tile(inner, f)
        own = i < s if side == 0 else i >= 4 - s
        return jnp.where(own, turn(tile(inner, f), inward * (s - 4)), turn(tile(outer, f), inward * s))

    def moved(x, n):
        keep = i >= n if side == 0 else i < 4 - n
        return jnp.where(keep, turn(x, inward * n), 0.0)

    q, p, b = tile(nxt if side == 0 else prv, 0), rows(1, 0), rows(3, 0)
    here = weights(rows(4, 0), rows(5, 0), rows(6, 0))
    for s in range(STEPS):
        if s == STEPS // 2:
            middle = q
            p = p + moved(rows(2, 0), 2)
        there = weights(rows(4, s + 1), rows(5, s + 1), rows(6, s + 1))
        a0, ae, aw, an, as_ = there
        ahead, behind = (ae, aw) if side == 0 else (aw, ae)
        mid = moved(q, 1)
        past = moved(q, 2)
        if s < STEPS - 1:
            past = past + feed[side, 0, s, m]
        q = a0 * mid + ahead * q + behind * past + an * north(mid) + as_ * south(mid)
        ahead, behind = (here[2], here[1]) if side == 0 else (here[1], here[2])
        out = []
        for run, x in ((1, p), (2, b)):
            y = moved(along_y(x, here), 1) + ahead * x + moved(behind * x, 2)
            if s < STEPS - 1:
                y = y + feed[side, run, s, m]
            out.append(y)
        p, b = out
        here = there
    return middle, q, p, b


def outer_kernel(first, last, nxt, prv, fixed, states, resid, inverse, feed, send, zobs, part):
    row = lax.broadcasted_iota(jnp.int32, (8, NY), 0)
    cross = jnp.zeros((8, NY), F32)
    square = jnp.zeros((8, NY), F32)
    for m in range(2):
        more = [added(side, m, first, last, nxt, prv, feed) for side in range(2)]
        for h in range(2):
            l = 2 * m + h
            for k in range(4):
                rows = slice(8 * k, 8 * k + 8)
                tiles = [states[n, l, rows, :] for n in range(4)]
                if k == 0:
                    mid, *end = more[1]
                    tiles[0] = tiles[0] + jnp.where(row < 2, turn(mid, -2 - 4 * h), 0.0)
                    for n in range(3):
                        tiles[n + 1] = tiles[n + 1] + jnp.where(row < 4, turn(end[n], -4 * h), 0.0)
                if k == 3:
                    mid, *end = more[0]
                    tiles[0] = tiles[0] + jnp.where(row >= 6, turn(mid, 6 - 4 * h), 0.0)
                    for n in range(3):
                        tiles[n + 1] = tiles[n + 1] + jnp.where(row >= 4, turn(end[n], 4 - 4 * h), 0.0)
                t = OUT_AT[4 * l + k]
                send[t, 0:8, :] = fixed[l, rows, :]
                for n in range(1, 4):
                    send[t, 8 * n : 8 * n + 8, :] = tiles[n]
                for j in range(2):
                    r = resid[j, l, rows, :] - tiles[j]
                    z = r * inverse[j, l, rows, :]
                    zobs[j, l, rows, :] = z
                    cross = cross + r * z
                    square = square + z * z
    part[0] = cross
    part[1] = square


def sum_kernel(count, recv, part, back, out):
    cross, square = part[0], part[1]
    z = jnp.zeros((8, NY), F32)
    before = jnp.zeros((8, NY), F32)
    for w in range(NW):
        i, o = OUT_AT[w], BACK_AT[w]
        r = recv[i, 0:8, :] + before
        before = recv[i, 8:16, :]
        z = z + r
        cross = cross + r * z
        square = square + z * z
        back[o, 0:8, :] = z[:, :HALF]
        back[o, 8:16, :] = z[:, HALF:]
    z = jnp.zeros((8, NY), F32)
    after = jnp.zeros((8, NY), F32)
    for w in reversed(range(NW)):
        i, o = OUT_AT[w], BACK_AT[w]
        r = after - recv[i, 16:24, :]
        after = recv[i, 24:32, :]
        z = z + r
        cross = cross + r * z
        square = square + z * z
        back[o, 16:24, :] = z[:, :HALF]
        back[o, 24:32, :] = z[:, HALF:]

    def fold(v):
        v = v[:, :HALF] + v[:, HALF:]
        return v + pltpu.roll(v, HALF // 2, 1)

    lane = lax.broadcasted_iota(jnp.int32, (8, HALF), 1)
    both = jnp.where(lane < HALF // 2, fold(cross), fold(square))
    row = jnp.sum(both, axis=0, keepdims=True)
    for s in range(count):
        out[s] = row


def join_kernel(count, sums, back, out):
    total = sums[0]
    for s in range(1, count):
        total = total + sums[s]
    tile = jnp.broadcast_to(total, (8, HALF))
    for w in range(NW):
        out[w, 0:32, :] = back[w]
        out[w, 32:40, :] = tile


def update_kernel(recv, lag, obs, inc, zobs, lag_out, obs_out, inc_out):
    total = recv[0, 32:33, :]
    for w in range(1, NW):
        total = total + recv[w, 32:33, :]
    lane = lax.broadcasted_iota(jnp.int32, (1, HALF), 1)
    cross = jnp.sum(jnp.where(lane < HALF // 2, total, 0.0), axis=1, keepdims=True)
    square = jnp.sum(jnp.where(lane < HALF // 2, 0.0, total), axis=1, keepdims=True)
    step = cross / (square + 1e-06)
    for l in range(LEV):
        for k in range(4):
            rows = slice(8 * k, 8 * k + 8)
            t = BACK_AT[4 * l + k]
            for h in range(2):
                cols = slice(HALF * h, HALF * h + HALF)
                lag_out[0, l, rows, cols] = lag[0, l, rows, cols] + step * recv[t, 8 * h : 8 * h + 8, :]
                inc_out[0, l, rows, cols] = inc[0, l, rows, cols] + step * recv[t, 16 + 8 * h : 24 + 8 * h, :]
        for j in range(2):
            obs_out[0, j, l] = obs[0, j, l] + step * zobs[j, l]


def body(lag, obs, inc, mside, oside, mvar, ovar, cx, cy, df):
    sds = jax.ShapeDtypeStruct
    size = lax.axis_size("space")
    edge = sds((EDGE * LEV * 4, NY), F32)
    one, two, four = (sds(n + (LEV, ROWS, NY), F32) for n in ((), (2,), (4,)))
    feed = sds((2, 3, STEPS - 1, LEV // 2, 8, NY), F32)
    held = [pltpu.with_memory_space_constraint(x, pltpu.HBM) for x in (lag, obs, inc, mside, oside, mvar, ovar, cx, cy, df)]
    first, last = call(
        edge_kernel,
        (edge, edge),
        [ANY] * 6,
        (VMEM,) * 2,
        [pltpu.VMEM((EDGE, LEV, 8, NY), F32)] * 2 + [pltpu.SemaphoreType.DMA((2 * EDGE,))],
        name="edges",
    )(*held[:3], *held[7:])
    nxt = lax.ppermute(first, "space", [((i + 1) % size, i) for i in range(size)])
    prv = lax.ppermute(last, "space", [(i, (i + 1) % size) for i in range(size)])
    inner = call(
        inner_kernel,
        (one, four, two, two, feed),
        [VMEM] * 10,
        (VMEM,) * 5,
        name="inner_runs",
        cost_estimate=pl.CostEstimate(flops=8 * 1024 * 1024, bytes_accessed=4 * 1024 * 1024, transcendentals=0),
    )(*held)
    send, zobs, part = call(
        outer_kernel,
        (sds((NW, 32, NY), F32), two, sds((2, 8, NY), F32)),
        [VMEM] * 9,
        (VMEM, VMEM, VMEM),
        name="outer_runs",
    )(first, last, nxt, prv, *inner)
    recv = lax.all_to_all(send, "tm", 0, 0, axis_index_groups=[OUT_ORDER])
    back, sums = call(
        functools.partial(sum_kernel, size),
        (sds((NW, 32, HALF), F32), sds((size, 1, HALF), F32)),
        [VMEM] * 2,
        (VMEM, VMEM),
        name="window_sums",
    )(recv, part)
    sums = lax.all_to_all(sums, "space", 0, 0, axis_index_groups=[SPACE_ORDER])
    back = call(
        functools.partial(join_kernel, size),
        sds((NW, 40, HALF), F32),
        [VMEM] * 2,
        VMEM,
        name="join",
    )(sums, back)
    back = lax.all_to_all(back, "tm", 0, 0, axis_index_groups=[BACK_ORDER])
    return call(
        update_kernel,
        (sds(lag.shape, F32), sds(obs.shape, F32), sds(inc.shape, F32)),
        [VMEM] * 5,
        (VMEM, VMEM, VMEM),
        name="update",
    )(back, lag, obs, inc, zobs)


def solution(mesh):
    field = P("tm", None, "space", None)
    pair = P("tm", None, None, "space", None)
    coef = P(None, "space", None)
    return jax.shard_map(
        body,
        mesh=mesh,
        in_specs=(field, pair, field, field, pair, field, pair, coef, coef, coef),
        out_specs=(field, pair, field),
        check_vma=False,
    )
```

```python
import functools

import jax
import jax.numpy as jnp
from jax import lax
from jax.experimental import pallas as pl
from jax.experimental.pallas import tpu as pltpu
from jax.sharding import PartitionSpec as P

STEPS = 4
LEV = 4
ROWS = 32
NY = 256
NW = 16
HALF = 128
EDGE = 7
F32 = jnp.float32

SPACE_ORDER = [2 * (z % 16) + core for z in range(26, 10, -1) for core in (1, 0)]
OUT_ORDER = [10, 6, 9, 11, 14, 2, 5, 7, 8, 13, 15, 1, 3, 4, 12, 0]
BACK_ORDER = OUT_ORDER
OUT_AT = [OUT_ORDER.index(w) for w in range(NW)]
BACK_AT = [BACK_ORDER.index(w) for w in range(NW)]

VMEM = pl.BlockSpec(memory_space=pltpu.VMEM)
ANY = pl.BlockSpec(memory_space=pl.ANY)


def call(kernel, out_shape, in_specs, out_specs, scratch=(), **kw):
    return pl.pallas_call(
        kernel,
        out_shape=out_shape,
        in_specs=in_specs,
        out_specs=out_specs,
        scratch_shapes=list(scratch),
        compiler_params=pltpu.CompilerParams(vmem_limit_bytes=16 * 1024 * 1024),
        **kw,
    )


def edge_kernel(lag, obs, inc, cx, cy, df, first_out, last_out, first, last, sem):
    sources = [inc.at[0], obs.at[0, 1], obs.at[0, 0], lag.at[0], cx, cy, df]
    copies = []
    for f, src in enumerate(sources):
        copies.append(pltpu.make_async_copy(src.at[:, pl.ds(0, 8)], first.at[f], sem.at[2 * f]))
        copies.append(pltpu.make_async_copy(src.at[:, pl.ds(ROWS - 8, 8)], last.at[f], sem.at[2 * f + 1]))
    for c in copies:
        c.start()
    for c in copies:
        c.wait()
    low = lax.broadcasted_iota(jnp.int32, (8, NY), 0) < 4
    for f in range(EDGE):
        for m in range(2):
            k = 8 * (2 * f + m)
            first_out[k : k + 8, :] = jnp.where(low, first[f, 2 * m], pltpu.roll(first[f, 2 * m + 1], 4, 0))
            last_out[k : k + 8, :] = jnp.where(low, pltpu.roll(last[f, 2 * m], 4, 0), last[f, 2 * m + 1])


def turn(x, rows):
    return pltpu.roll(x, rows % x.shape[0], 0)


def north(x):
    return pltpu.roll(x, NY - 1, 1)


def south(x):
    return pltpu.roll(x, 1, 1)


def weights(cx, cy, df):
    col = lax.broadcasted_iota(jnp.int32, df.shape, 1)
    x, y = 0.5 * cx, 0.5 * cy
    an = jnp.where(col == NY - 1, 0.0, df - y)
    as_ = jnp.where(col == 0, 0.0, df + y)
    return 1.0 - 4.0 * df, df - x, df + x, an, as_


def along_y(p, c):
    return c[0] * p + north(c[4] * p) + south(c[3] * p)


def inner_kernel(lag, obs, inc, mside, oside, mvar, ovar, cx, cy, df, fixed, states, resid, inverse, feed):
    tile_row = lax.broadcasted_iota(jnp.int32, (8, NY), 0)
    row = lax.broadcasted_iota(jnp.int32, (ROWS, NY), 0)

    def hand_over(l, run, step, up, down):
        m, h = l // 2, 4 * (l % 2)
        for side, (x, at, to) in enumerate(((up, 7, h + step + 1), (down, 0, h + 2 - step))):
            other = 0.0 if h == 0 else feed[side, run, step, m]
            feed[side, run, step, m] = jnp.where(tile_row == to, turn(x, to - at), other)

    for l in range(LEV):
        a0, ae_full, aw_full, an, as_ = c = weights(cx[l], cy[l], df[l])
        ae = jnp.where(row == ROWS - 1, 0.0, ae_full)
        aw = jnp.where(row == 0, 0.0, aw_full)
        lagr = lag[0, l]
        q, p, b = inc[0, l], obs[0, 1, l], lagr
        for step in range(STEPS):
            if step == STEPS // 2:
                states[0, l] = q
                p = p + obs[0, 0, l]
            if step < STEPS - 1:
                hand_over(l, 0, step, q[ROWS - 8 :], q[:8])
                for run, x in ((1, p), (2, b)):
                    hand_over(l, run, step, ae_full[ROWS - 8 :] * x[ROWS - 8 :], aw_full[:8] * x[:8])
            q = a0 * q + ae * turn(q, -1) + aw * turn(q, 1) + an * north(q) + as_ * south(q)
            p = along_y(p, c) + turn(aw * p, -1) + turn(ae * p, 1)
            b = along_y(b, c) + turn(aw * b, -1) + turn(ae * b, 1)
        states[1, l] = q
        states[2, l] = p + lagr
        states[3, l] = b
        fixed[l] = mside[0, l] - mvar[0, l] * lagr - inc[0, l]
        for j in range(2):
            var = ovar[0, j, l]
            resid[j, l] = oside[0, j, l] - var * obs[0, j, l]
            inverse[j, l] = 1.0 / var


def added(side, m, first, last, nxt, prv, feed):
    i = lax.broadcasted_iota(jnp.int32, (8, NY), 0) & 3
    inward = 1 - 2 * side

    def tile(ref, f):
        k = 8 * (2 * f + m)
        return ref[k : k + 8, :]

    def rows(f, s):
        outer, inner = (nxt, last) if side == 0 else (prv, first)
        if s == 0:
            return tile(outer, f)
        if s == 4:
            return tile(inner, f)
        own = i < s if side == 0 else i >= 4 - s
        return jnp.where(own, turn(tile(inner, f), inward * (s - 4)), turn(tile(outer, f), inward * s))

    def moved(x, n):
        keep = i >= n if side == 0 else i < 4 - n
        return jnp.where(keep, turn(x, inward * n), 0.0)

    q, p, b = tile(nxt if side == 0 else prv, 0), rows(1, 0), rows(3, 0)
    here = weights(rows(4, 0), rows(5, 0), rows(6, 0))
    for s in range(STEPS):
        if s == STEPS // 2:
            middle = q
            p = p + moved(rows(2, 0), 2)
        there = weights(rows(4, s + 1), rows(5, s + 1), rows(6, s + 1))
        a0, ae, aw, an, as_ = there
        ahead, behind = (ae, aw) if side == 0 else (aw, ae)
        mid = moved(q, 1)
        past = moved(q, 2)
        if s < STEPS - 1:
            past = past + feed[side, 0, s, m]
        q = a0 * mid + ahead * q + behind * past + an * north(mid) + as_ * south(mid)
        ahead, behind = (here[2], here[1]) if side == 0 else (here[1], here[2])
        out = []
        for run, x in ((1, p), (2, b)):
            y = moved(along_y(x, here), 1) + ahead * x + moved(behind * x, 2)
            if s < STEPS - 1:
                y = y + feed[side, run, s, m]
            out.append(y)
        p, b = out
        here = there
    return middle, q, p, b


def outer_kernel(first, last, nxt, prv, fixed, states, resid, inverse, feed, send, zobs, part):
    row = lax.broadcasted_iota(jnp.int32, (8, NY), 0)
    cross = jnp.zeros((8, NY), F32)
    square = jnp.zeros((8, NY), F32)
    for m in range(2):
        more = [added(side, m, first, last, nxt, prv, feed) for side in range(2)]
        for h in range(2):
            l = 2 * m + h
            for k in range(4):
                rows = slice(8 * k, 8 * k + 8)
                tiles = [states[n, l, rows, :] for n in range(4)]
                if k == 0:
                    mid, *end = more[1]
                    tiles[0] = tiles[0] + jnp.where(row < 2, turn(mid, -2 - 4 * h), 0.0)
                    for n in range(3):
                        tiles[n + 1] = tiles[n + 1] + jnp.where(row < 4, turn(end[n], -4 * h), 0.0)
                if k == 3:
                    mid, *end = more[0]
                    tiles[0] = tiles[0] + jnp.where(row >= 6, turn(mid, 6 - 4 * h), 0.0)
                    for n in range(3):
                        tiles[n + 1] = tiles[n + 1] + jnp.where(row >= 4, turn(end[n], 4 - 4 * h), 0.0)
                t = OUT_AT[4 * l + k]
                send[t, 0:8, :] = fixed[l, rows, :]
                for n in range(1, 4):
                    send[t, 8 * n : 8 * n + 8, :] = tiles[n]
                for j in range(2):
                    r = resid[j, l, rows, :] - tiles[j]
                    z = r * inverse[j, l, rows, :]
                    zobs[j, l, rows, :] = z
                    cross = cross + r * z
                    square = square + z * z
    part[0] = cross
    part[1] = square


def sum_kernel(count, recv, part, back, out):
    cross, square = part[0], part[1]
    z = jnp.zeros((8, NY), F32)
    before = jnp.zeros((8, NY), F32)
    for w in range(NW):
        i, o = OUT_AT[w], BACK_AT[w]
        r = recv[i, 0:8, :] + before
        before = recv[i, 8:16, :]
        z = z + r
        cross = cross + r * z
        square = square + z * z
        back[o, 0:8, :] = z[:, :HALF]
        back[o, 8:16, :] = z[:, HALF:]
    z = jnp.zeros((8, NY), F32)
    after = jnp.zeros((8, NY), F32)
    for w in reversed(range(NW)):
        i, o = OUT_AT[w], BACK_AT[w]
        r = after - recv[i, 16:24, :]
        after = recv[i, 24:32, :]
        z = z + r
        cross = cross + r * z
        square = square + z * z
        back[o, 16:24, :] = z[:, :HALF]
        back[o, 24:32, :] = z[:, HALF:]

    def fold(v):
        v = v[:, :HALF] + v[:, HALF:]
        return v + pltpu.roll(v, HALF // 2, 1)

    lane = lax.broadcasted_iota(jnp.int32, (8, HALF), 1)
    both = jnp.where(lane < HALF // 2, fold(cross), fold(square))
    row = jnp.sum(both, axis=0, keepdims=True)
    for s in range(count):
        out[s] = row


def join_kernel(count, sums, back, out):
    total = sums[0]
    for s in range(1, count):
        total = total + sums[s]
    tile = jnp.broadcast_to(total, (8, HALF))
    for w in range(NW):
        out[w, 0:32, :] = back[w]
        out[w, 32:40, :] = tile


def update_kernel(recv, lag, obs, inc, zobs, lag_out, obs_out, inc_out):
    total = recv[0, 32:33, :]
    for w in range(1, NW):
        total = total + recv[w, 32:33, :]
    lane = lax.broadcasted_iota(jnp.int32, (1, HALF), 1)
    cross = jnp.sum(jnp.where(lane < HALF // 2, total, 0.0), axis=1, keepdims=True)
    square = jnp.sum(jnp.where(lane < HALF // 2, 0.0, total), axis=1, keepdims=True)
    step = cross / (square + 1e-06)
    for l in range(LEV):
        for k in range(4):
            rows = slice(8 * k, 8 * k + 8)
            t = BACK_AT[4 * l + k]
            for h in range(2):
                cols = slice(HALF * h, HALF * h + HALF)
                lag_out[0, l, rows, cols] = lag[0, l, rows, cols] + step * recv[t, 8 * h : 8 * h + 8, :]
                inc_out[0, l, rows, cols] = inc[0, l, rows, cols] + step * recv[t, 16 + 8 * h : 24 + 8 * h, :]
        for j in range(2):
            obs_out[0, j, l] = obs[0, j, l] + step * zobs[j, l]


def body(lag, obs, inc, mside, oside, mvar, ovar, cx, cy, df):
    sds = jax.ShapeDtypeStruct
    size = lax.axis_size("space")
    edge = sds((EDGE * LEV * 4, NY), F32)
    one, two, four = (sds(n + (LEV, ROWS, NY), F32) for n in ((), (2,), (4,)))
    feed = sds((2, 3, STEPS - 1, LEV // 2, 8, NY), F32)
    held = [pltpu.with_memory_space_constraint(x, pltpu.HBM) for x in (lag, obs, inc, mside, oside, mvar, ovar, cx, cy, df)]
    first, last = call(
        edge_kernel,
        (edge, edge),
        [ANY] * 6,
        (VMEM,) * 2,
        [pltpu.VMEM((EDGE, LEV, 8, NY), F32)] * 2 + [pltpu.SemaphoreType.DMA((2 * EDGE,))],
        name="edges",
    )(*held[:3], *held[7:])
    prv = lax.ppermute(last, "space", [(i, (i + 1) % size) for i in range(size)])
    nxt = lax.ppermute(first, "space", [((i + 1) % size, i) for i in range(size)])
    inner = call(
        inner_kernel,
        (one, four, two, two, feed),
        [VMEM] * 10,
        (VMEM,) * 5,
        name="inner_runs",
        cost_estimate=pl.CostEstimate(flops=8 * 1024 * 1024, bytes_accessed=4 * 1024 * 1024, transcendentals=0),
    )(*held)
    send, zobs, part = call(
        outer_kernel,
        (sds((NW, 32, NY), F32), two, sds((2, 8, NY), F32)),
        [VMEM] * 9,
        (VMEM, VMEM, VMEM),
        name="outer_runs",
    )(first, last, nxt, prv, *inner)
    recv = lax.all_to_all(send, "tm", 0, 0, axis_index_groups=[OUT_ORDER])
    back, sums = call(
        functools.partial(sum_kernel, size),
        (sds((NW, 32, HALF), F32), sds((size, 1, HALF), F32)),
        [VMEM] * 2,
        (VMEM, VMEM),
        name="window_sums",
    )(recv, part)
    sums = lax.all_to_all(sums, "space", 0, 0, axis_index_groups=[SPACE_ORDER])
    back = call(
        functools.partial(join_kernel, size),
        sds((NW, 40, HALF), F32),
        [VMEM] * 2,
        VMEM,
        name="join",
    )(sums, back)
    back = lax.all_to_all(back, "tm", 0, 0, axis_index_groups=[BACK_ORDER])
    return call(
        update_kernel,
        (sds(lag.shape, F32), sds(obs.shape, F32), sds(inc.shape, F32)),
        [VMEM] * 5,
        (VMEM, VMEM, VMEM),
        name="update",
    )(back, lag, obs, inc, zobs)


def solution(mesh):
    field = P("tm", None, "space", None)
    pair = P("tm", None, None, "space", None)
    coef = P(None, "space", None)
    return jax.shard_map(
        body,
        mesh=mesh,
        in_specs=(field, pair, field, field, pair, field, pair, coef, coef, coef),
        out_specs=(field, pair, field),
        check_vma=False,
    )
```
